256 devices in a mesh: blk: 32 (over y_lo, z, core), rep: 8 (over y_hi, x).
Axes of the slice: x: 4, y: 4 (y_hi: 2, y_lo: 2; y = y_hi * 2 + y_lo), z: 8, core: 2. Of those that a mesh axis runs over, the one named last changes fastest.
Arguments:
- query_act: bfloat16 [16384, 16384], P('blk', 'rep'), may hold values from -8 to 8
- passage_act: bfloat16 [1024, 16384], P('blk', 'rep'), may hold values from -8 to 8
- positive: int32 [16384], P('blk'), may hold values from 0 to 1023
- normalizer: float32 [16384], P('blk'), as said below
Outputs:
- query_grad: bfloat16 [16384, 16384], P('blk', 'rep')
- passage_grad: bfloat16 [1024, 16384], P('blk', 'rep')
The draws below stay inside these ranges and needn't reach their ends.
Inputs may be any that keep to these rules, and one draw needn't show every extreme that they name: `normalizer`: close to the log of the sum over passages of exp(scores).
All inputs are finite; a program needn't handle non-finite values.
Results may differ from the reference program's by a relative error of at most 0.009.
The reference program's roundings to bfloat16 on the way (of `query_rep`, `passage_rep` and `score_grad`) count: a program that leaves them out, or rounds other values in their place, can miss the bound.
Values may be sent and summed in bfloat16 or wider, within the bound.
No kernel may reach another device: no remote copies, remote signals or barrier semaphores. Data moves between devices by JAX's collectives and lax.ppermute only.
A program may use at most 64 MiB of HBM per device.

```python
import math
import jax
import jax.numpy as jnp
from jax import lax

VOCAB = 16384
NQ = 16384
NP = 1024


def impact_pair(key):
    column_key = jax.random.fold_in(key, 13)
    query_key = jax.random.fold_in(key, 11)
    passage_key = jax.random.fold_in(key, 12)
    column_scale = jnp.exp(jax.random.uniform(column_key, (VOCAB,), jnp.float32, math.log(0.5), math.log(2.0)))
    query_raw = jnp.clip(jax.random.normal(query_key, (NQ, VOCAB), jnp.float32), -6.0, 6.0)
    passage_raw = jnp.clip(jax.random.normal(passage_key, (NP, VOCAB), jnp.float32), -6.0, 6.0)
    query_vals = jnp.clip(query_raw * column_scale[None, :], -8.0, 8.0)
    passage_vals = jnp.clip(passage_raw * column_scale[None, :], -8.0, 8.0)
    return (query_vals, passage_vals)


def draw_query_act(key, part):
    query_vals, passage_vals = impact_pair(key)
    return query_vals.astype(jnp.bfloat16)


def draw_passage_act(key, part):
    query_vals, passage_vals = impact_pair(key)
    return passage_vals.astype(jnp.bfloat16)


def draw_normalizer(key, part):
    query_vals, passage_vals = impact_pair(key)
    key = jax.random.fold_in(key, 21)
    factor = 8.0 / math.sqrt(VOCAB)
    query_rep = jnp.log1p(jnp.maximum(query_vals.astype(jnp.bfloat16).astype(jnp.float32), 0.0))
    passage_rep = jnp.log1p(jnp.maximum(passage_vals.astype(jnp.bfloat16).astype(jnp.float32), 0.0))
    column_mean = jnp.mean(passage_rep, axis=0)
    column_var = jnp.maximum(jnp.mean(passage_rep * passage_rep, axis=0) - column_mean * column_mean, 0.0)
    centre = factor * jnp.dot(query_rep, column_mean, precision=lax.Precision.HIGHEST)
    spread_term = factor * factor * jnp.dot(query_rep * query_rep, column_var, precision=lax.Precision.HIGHEST)
    jitter = jax.random.uniform(key, (NQ,), jnp.float32, -0.5, 0.5)
    return centre + math.log(NP) + 0.5 * spread_term + jitter


def with_ends(result, stream_key, least, top_value):
    longest = result.shape.index(max(result.shape))
    spots = []
    for shift in (0, 1):
        where = [jax.random.randint(jax.random.fold_in(stream_key, axis), (), 0, length) for axis, length in enumerate(result.shape)]
        where[longest] = (where[longest] + shift) % result.shape[longest]
        spots.append(tuple(where))
    return result.at[spots[0]].set(least).at[spots[1]].set(top_value)


def setup_inputs(seed: int = 0) -> dict:
    key_list = jax.random.split(jax.random.key(seed), 5)
    return {
        "query_act": draw_query_act(jax.random.fold_in(key_list[4], 71), 0),
        "passage_act": draw_passage_act(jax.random.fold_in(key_list[4], 71), 0),
        "positive": with_ends(jax.random.randint(key_list[2], (NQ,), 0, NP), jax.random.fold_in(key_list[2], 1), 0, NP - 1).astype(jnp.int32),
        "normalizer": draw_normalizer(jax.random.fold_in(key_list[4], 71), 0),
    }


def saturate(act):
    wide = act.astype(jnp.float32)
    return jnp.log1p(jnp.maximum(wide, 0.0))

def slope(act):
    wide = act.astype(jnp.float32)
    return jnp.where(wide > 0.0, 1.0 / (1.0 + jnp.maximum(wide, 0.0)), 0.0)

def reference(query_act, passage_act, positive, normalizer):
    factor = 8.0 / math.sqrt(VOCAB)
    query_rep = saturate(query_act).astype(jnp.bfloat16)
    passage_rep = saturate(passage_act).astype(jnp.bfloat16)
    scores = jnp.dot(query_rep, passage_rep.T, preferred_element_type=jnp.float32) * factor
    columns = jnp.arange(NP, dtype=jnp.int32)
    onehot = (positive[:, None] == columns[None, :]).astype(jnp.float32)
    score_grad = ((jnp.exp(scores - normalizer[:, None]) - onehot) * (8.0 * factor)).astype(jnp.bfloat16)
    query_sum = jnp.dot(score_grad, passage_rep, preferred_element_type=jnp.float32)
    query_grad = (query_sum * slope(query_act)).astype(jnp.bfloat16)
    passage_sum = lax.dot_general(score_grad, query_rep, (((0,), (0,)), ((), ())), preferred_element_type=jnp.float32)
    passage_grad = (passage_sum * slope(passage_act)).astype(jnp.bfloat16)
    return (query_grad, passage_grad)
```

```python
import math

import jax
import jax.numpy as jnp
from jax import lax
from jax.sharding import Mesh, PartitionSpec as P

VOCAB = 16384
REP = ("yhi", "x")


def saturate(act):
    wide = act.astype(jnp.float32)
    return jnp.log1p(jnp.maximum(wide, 0.0)).astype(jnp.bfloat16)


def slope(act):
    wide = act.astype(jnp.float32)
    return jnp.where(wide > 0.0, 1.0 / (1.0 + jnp.maximum(wide, 0.0)), 0.0)


def swap(value, axis):
    return lax.ppermute(value, axis, [(0, 1), (1, 0)])


def shift(value, step):
    return lax.ppermute(value, "z", [(i, (i + step) % 8) for i in range(8)])


def shards(query_act, passage_act, positive, normalizer):
    factor = 8.0 / math.sqrt(VOCAB)
    core, y, z = lax.axis_index("core"), lax.axis_index("ylo"), lax.axis_index("z")
    rep = lax.axis_index(REP)
    bf16, f32 = jnp.bfloat16, jnp.float32

    own = saturate(passage_act)
    blocks = {0: jnp.concatenate([own, swap(own, "ylo")], axis=0)}
    for d in range(1, 4):
        blocks[-d] = shift(blocks[1 - d], 1)
        blocks[d] = shift(blocks[d - 1], -1)
    blocks[4] = jnp.concatenate([shift(blocks[-3][:32], 1), shift(blocks[3][32:], -1)], axis=0)
    order = [0, 1, -1, 2, -2, 3, -3, 4]
    half = jnp.concatenate([blocks[d] for d in order], axis=0)

    query_rep = saturate(query_act)
    queries = jnp.concatenate([query_rep, swap(query_rep, "core")], axis=0)
    row_info = jnp.stack([normalizer, positive.astype(f32)])
    row_info = jnp.concatenate([row_info, swap(row_info, "core")], axis=1)
    row_info = lax.dynamic_slice_in_dim(row_info, rep * 128, 128, axis=1)

    part = lax.dot_general(queries, half, (((1,), (1,)), ((), ())), preferred_element_type=f32)
    pieces = lax.all_to_all(part.reshape(8, 128, 512), REP, split_axis=0, concat_axis=0)
    scores = jnp.sum(pieces, axis=0) * factor

    place = jnp.arange(512, dtype=jnp.int32)
    where = jnp.array(order, dtype=jnp.int32)[place // 64]
    ident = jnp.where(place % 64 < 32, y, 1 - y) * 16 + ((z + where + 8) % 8) * 2 + core
    ident = ident * 32 + place % 32
    onehot = (row_info[1].astype(jnp.int32)[:, None] == ident[None, :]).astype(f32)
    score_grad = ((jnp.exp(scores - row_info[0][:, None]) - onehot) * (8.0 * factor)).astype(bf16)
    spread = lax.all_to_all(
        jnp.broadcast_to(score_grad[None], (8, 128, 512)), REP, split_axis=0, concat_axis=0
    ).reshape(1024, 512)

    def term(d):
        at = order.index(d) * 64
        return lax.dot_general(
            spread[:, at : at + 64], queries, (((0,), (0,)), ((), ())), preferred_element_type=f32
        )

    far = term(4).astype(bf16)
    up, down = shift(far[:32], 1), shift(far[32:], -1)
    for d in (3, 2, 1):
        mine_up, mine_down = term(d), term(-d)
        if d == 3:
            pad = jnp.zeros((32, mine_up.shape[1]), f32)
            up = jnp.concatenate([up.astype(f32), pad], axis=0)
            down = jnp.concatenate([pad, down.astype(f32)], axis=0)
        up = shift((mine_up + up.astype(f32)).astype(bf16), 1)
        down = shift((mine_down + down.astype(f32)).astype(bf16), -1)
    total = term(0) + up.astype(f32) + down.astype(f32)
    passage_sum = total[:32] + swap(total[32:].astype(bf16), "ylo").astype(f32)
    passage_grad = (passage_sum * slope(passage_act)).astype(bf16)

    other_half = swap(half, "core")
    other_grad = swap(spread[512:], "core")
    query_sum = jnp.dot(spread[:512], half, preferred_element_type=f32) + jnp.dot(
        other_grad, other_half, preferred_element_type=f32
    )
    query_grad = (query_sum * slope(query_act)).astype(bf16)
    return (query_grad, passage_grad)


def solution(mesh):
    split = Mesh(mesh.devices.reshape(2, 8, 2, 2, 4), ("ylo", "z", "core", "yhi", "x"))
    rows, columns = ("ylo", "z", "core"), ("yhi", "x")
    return jax.shard_map(
        shards,
        mesh=split,
        in_specs=(P(rows, columns), P(rows, columns), P(rows), P(rows)),
        out_specs=(P(rows, columns), P(rows, columns)),
        check_vma=False,
    )
```

```python
import math

import jax
import jax.numpy as jnp
from jax import lax
from jax.sharding import Mesh, PartitionSpec as P

VOCAB = 16384
REP = ("yhi", "x")
NEAR = [(0, 0), (1, 0), (0, 1), (1, 1), (0, -1), (1, -1), (0, 2), (0, -2)]
FAR = [(1, 2), (1, -2), (0, 3), (0, -3), (1, 3), (1, -3), (0, 4), (1, 4)]


def saturate(act):
    wide = act.astype(jnp.float32)
    return jnp.log1p(jnp.maximum(wide, 0.0)).astype(jnp.bfloat16)


def slope(act):
    wide = act.astype(jnp.float32)
    return jnp.where(wide > 0.0, 1.0 / (1.0 + jnp.maximum(wide, 0.0)), 0.0)


def swap(value, axis):
    return lax.ppermute(value, axis, [(0, 1), (1, 0)])


def shift(value, step):
    return lax.ppermute(value, "z", [(i, (i + step) % 8) for i in range(8)])


def shards(query_act, passage_act, positive, normalizer):
    factor = 8.0 / math.sqrt(VOCAB)
    core, y, z = lax.axis_index("core"), lax.axis_index("ylo"), lax.axis_index("z")
    rep = lax.axis_index(REP)
    bf16, f32 = jnp.bfloat16, jnp.float32

    own = saturate(passage_act)
    blocks = {(0, 0): own, (1, 0): swap(own, "ylo")}
    for d in range(1, 4):
        for s in (0, 1):
            blocks[s, -d] = shift(blocks[s, 1 - d], 1)
            blocks[s, d] = shift(blocks[s, d - 1], -1)
    blocks[0, 4] = shift(blocks[0, -3], 1)
    blocks[1, 4] = shift(blocks[1, 3], -1)

    query_rep = saturate(query_act)
    queries = jnp.concatenate([query_rep, swap(query_rep, "core")], axis=0)
    row_info = jnp.stack([normalizer, positive.astype(f32)])
    row_info = jnp.concatenate([row_info, swap(row_info, "core")], axis=1)
    row_info = lax.dynamic_slice_in_dim(row_info, rep * 128, 128, axis=1)
    row_norm, row_positive = row_info[0][:, None], row_info[1].astype(jnp.int32)[:, None]

    def spread_grad(keys, passages):
        part = lax.dot_general(queries, passages, (((1,), (1,)), ((), ())), preferred_element_type=f32)
        pieces = lax.all_to_all(part.reshape(8, 128, 256), REP, split_axis=0, concat_axis=0)
        scores = jnp.sum(pieces, axis=0) * factor
        place = jnp.arange(256, dtype=jnp.int32)
        stream = jnp.array([s for s, _ in keys], dtype=jnp.int32)[place // 32]
        where = jnp.array([d for _, d in keys], dtype=jnp.int32)[place // 32]
        ident = ((y + stream) % 2) * 16 + ((z + where + 8) % 8) * 2 + core
        ident = ident * 32 + place % 32
        onehot = (row_positive == ident[None, :]).astype(f32)
        grad = ((jnp.exp(scores - row_norm) - onehot) * (8.0 * factor)).astype(bf16)
        return lax.all_to_all(
            jnp.broadcast_to(grad[None], (8, 128, 256)), REP, split_axis=0, concat_axis=0
        ).reshape(1024, 256)

    near = jnp.concatenate([blocks[k] for k in NEAR], axis=0)
    far = jnp.concatenate([blocks[k] for k in FAR], axis=0)
    near_grad = spread_grad(NEAR, near)
    far_grad = spread_grad(FAR, far)

    def sums(grad):
        return lax.dot_general(grad, queries, (((0,), (0,)), ((), ())), preferred_element_type=f32)

    terms = {}
    for keys, block in ((FAR, sums(far_grad)), (NEAR, sums(near_grad))):
        block = lax.optimization_barrier(block)
        for i, k in enumerate(keys):
            terms[k] = block[i * 32 : i * 32 + 32]

    up, down = {}, {}
    up[0] = shift(terms[0, 4].astype(bf16), 1).astype(f32)
    down[1] = shift(terms[1, 4].astype(bf16), -1).astype(f32)
    up[1] = down[0] = 0.0
    for d in (3, 2, 1):
        for s in (1, 0):
            up[s] = shift((terms[s, d] + up[s]).astype(bf16), 1).astype(f32)
            down[s] = shift((terms[s, -d] + down[s]).astype(bf16), -1).astype(f32)
    partner = swap((terms[1, 0] + up[1] + down[1]).astype(bf16), "ylo").astype(f32)
    passage_sum = terms[0, 0] + up[0] + down[0] + partner
    passage_grad = (passage_sum * slope(passage_act)).astype(bf16)

    passages = jnp.concatenate([near, far, swap(near, "core"), swap(far, "core")], axis=0)
    grads = jnp.concatenate(
        [near_grad[:512], far_grad[:512], swap(near_grad[512:], "core"), swap(far_grad[512:], "core")],
        axis=1,
    )
    query_sum = jnp.dot(grads, passages, preferred_element_type=f32)
    query_grad = (query_sum * slope(query_act)).astype(bf16)
    return (query_grad, passage_grad)


def solution(mesh):
    split = Mesh(mesh.devices.reshape(2, 8, 2, 2, 4), ("ylo", "z", "core", "yhi", "x"))
    rows, columns = ("ylo", "z", "core"), ("yhi", "x")
    return jax.shard_map(
        shards,
        mesh=split,
        in_specs=(P(rows, columns), P(rows, columns), P(rows), P(rows)),
        out_specs=(P(rows, columns), P(rows, columns)),
        check_vma=False,
    )
```

```python
import functools
import math

import jax
import jax.numpy as jnp
from jax import lax
from jax.experimental import pallas as pl
from jax.experimental.pallas import tpu as pltpu
from jax.sharding import Mesh, PartitionSpec as P

VOCAB = 16384
REP = ("x", "yhi")
FACTOR = 8.0 / math.sqrt(VOCAB)
BF16, F32 = jnp.bfloat16, jnp.float32
ORDER = [4, 3, -3, 2, -2, 1, -1, 0]
KEYS = [(s, d) for d in ORDER for s in (0, 1)]
VMEM = pl.BlockSpec(memory_space=pltpu.VMEM)
ANY = pl.BlockSpec(memory_space=pl.ANY)
PARAMS = pltpu.CompilerParams(vmem_limit_bytes=16 * 1024 * 1024)


def shape(dims, dtype):
    return jax.ShapeDtypeStruct(dims, dtype)


def saturate(act):
    wide = jnp.maximum(act.astype(F32), 0.0)
    small = wide - 0.5 * wide * wide
    return jnp.where(wide < 2.0**-8, small, jnp.log(1.0 + wide)).astype(BF16)


def slope(act):
    wide = act.astype(F32)
    return jnp.where(wide > 0.0, 1.0 / (1.0 + jnp.maximum(wide, 0.0)), 0.0)


def swap(value, axis):
    return lax.ppermute(value, axis, [(0, 1), (1, 0)])


def shift(value, step):
    return lax.ppermute(value, "z", [(i, (i + step) % 8) for i in range(8)])


def exchange(value):
    return lax.all_to_all(value, REP, split_axis=0, concat_axis=0)


def after(value, *others):
    return lax.optimization_barrier((value, *others))[0]


def score_kernel(mine_ref, other_ref, *refs):
    blocks, out_ref, joined_ref = refs[:16], refs[-2], refs[-1]
    for i in range(16):
        joined_ref[i * 32 : i * 32 + 32, :] = blocks[i][...]
    for i, ref in enumerate((mine_ref, other_ref)):
        for k in range(2):
            part = lax.dot_general(
                joined_ref[...],
                ref[k * 256 : k * 256 + 256, :],
                (((1,), (1,)), ((), ())),
                preferred_element_type=F32,
            )
            most, least = jnp.max(part, axis=0, keepdims=True), jnp.min(part, axis=0, keepdims=True)
            halves = jnp.round(most + least)
            centre = halves * 0.5
            reach = jnp.maximum(most - centre, centre - least)
            step = jnp.maximum(jnp.ceil(reach * (2.0**17 / 32767)), 1.0)
            code = jnp.round((part - centre) * (2.0**17 / step))
            row = lax.broadcasted_iota(jnp.int32, (16, 256), 0)
            extra = jnp.where(row == 0, halves, jnp.where(row == 1, step, 0.0))
            for n in range(2):
                columns = slice(n * 128, n * 128 + 128)
                at = i * 4 + k * 2 + n
                out_ref[at, :512, :] = code[:, columns].astype(jnp.int32).astype(jnp.int16)
                out_ref[at, 512:, :] = extra[:, columns].astype(jnp.int32).astype(jnp.int16)


def partial_scores(mine, other, blocks):
    return pl.pallas_call(
        score_kernel,
        out_shape=(shape((8, 528, 128), jnp.int16), shape((512, 2048), BF16)),
        in_specs=[VMEM] * 18,
        out_specs=(VMEM, VMEM),
        compiler_params=PARAMS,
    )(mine, other, *blocks)


def grad_kernel(pieces_ref, norm_ref, other_norm_ref, at_ref, other_at_ref, out_ref):
    core, y, z = lax.axis_index("core"), lax.axis_index("ylo"), lax.axis_index("z")
    rep = lax.axis_index("x") * 2 + lax.axis_index("yhi")
    norm = jnp.where(rep < 4, norm_ref[...], other_norm_ref[...])
    positive = jnp.where(rep < 4, at_ref[...], other_at_ref[...])
    turn = lax.broadcasted_iota(jnp.int32, (4, 128), 0) == lax.rem(rep, 4)
    norm = jnp.sum(jnp.where(turn, norm, 0.0), axis=0, keepdims=True)
    positive = jnp.sum(jnp.where(turn, positive, 0), axis=0, keepdims=True)
    scores = 0.0
    for k in range(8):
        extra = pieces_ref[k, 512:, :].astype(jnp.int32).astype(F32)
        code = pieces_ref[k, :512, :].astype(jnp.int32).astype(F32)
        scores = scores + (code * (extra[1:2] * 2.0**-17) + extra[0:1] * 0.5)
    place = lax.broadcasted_iota(jnp.int32, (512, 128), 0)
    turn = place >> 6
    ahead = jnp.where((turn & 1) == 0, 4 + (turn >> 1), (7 - turn) >> 1)
    ident = ((y + (place >> 5)) & 1) * 512 + ((z + ahead) & 7) * 64 + core * 32 + (place & 31)
    onehot = (positive == ident).astype(F32)
    grad = (jnp.exp(scores * FACTOR - norm) - onehot) * (8.0 * FACTOR)
    grad = grad.astype(BF16)
    for k in range(8):
        out_ref[k] = grad


def score_grad(pieces, *rows):
    return pl.pallas_call(
        grad_kernel,
        out_shape=shape((8, 512, 128), BF16),
        in_specs=[VMEM] * 5,
        out_specs=VMEM,
        compiler_params=PARAMS,
    )(pieces, *rows)


def sum_kernel(at, grad_ref, mine_ref, other_ref, *refs):
    left = jnp.concatenate([grad_ref[k, at : at + 256, :] for k in range(8)], axis=1)
    for j in range(4):
        columns = slice(j * 512, j * 512 + 512)
        total = jnp.dot(left[:, :512], mine_ref[:, columns], preferred_element_type=F32)
        total += jnp.dot(left[:, 512:], other_ref[:, columns], preferred_element_type=F32)
        refs[-1][:, :, columns] = total.reshape(8, 32, 512)


def passage_sums(grad, mine, other, at, first):
    out = pl.pallas_call(
        functools.partial(sum_kernel, at),
        out_shape=shape((8, 32, 2048), F32),
        in_specs=[VMEM] * 3 + [ANY] * len(first),
        out_specs=VMEM,
        compiler_params=PARAMS,
    )(grad, mine, other, *first)
    return {k: out[i] for i, k in enumerate(KEYS[at // 32 : at // 32 + 8])}


def query_kernel(act_ref, own_grad_ref, other_grad_ref, own_ref, other_ref, out_ref, turned_ref):
    @pl.when(pl.program_id(0) == 0)
    def _():
        for i, g in enumerate((own_grad_ref, other_grad_ref)):
            for k in range(4):
                turned_ref[k * 128 : k * 128 + 128, i * 512 : i * 512 + 512] = g[k].T

    total = jnp.dot(turned_ref[:, :512], own_ref[...], preferred_element_type=F32)
    total += jnp.dot(turned_ref[:, 512:], other_ref[...], preferred_element_type=F32)
    wide = act_ref[...].astype(F32)
    below = 1.0 + jnp.maximum(wide, 0.0)
    guess = pl.reciprocal(below, approx=True)
    inverse = guess * (2.0 - below * guess)
    out_ref[...] = jnp.where(wide > 0.0, total * inverse, 0.0).astype(BF16)


def query_grads(act, grad, other_grad, own, other):
    column = pl.BlockSpec((512, 512), lambda j: (0, j))
    half = pl.BlockSpec((4, 512, 128), lambda j: (0, 0, 0))
    return pl.pallas_call(
        query_kernel,
        out_shape=shape((512, 2048), BF16),
        grid=(4,),
        in_specs=[column, half, half, column, column],
        out_specs=column,
        scratch_shapes=[pltpu.VMEM((512, 1024), BF16)],
        compiler_params=PARAMS,
    )(act, grad, other_grad, own, other)


def shards(query_act, passage_act, positive, normalizer):
    own = saturate(passage_act)
    blocks = {(0, 0): own, (1, 0): swap(own, "ylo")}
    for d in range(1, 4):
        for s in (0, 1):
            blocks[s, -d] = shift(blocks[s, 1 - d], 1)
            blocks[s, d] = shift(blocks[s, d - 1], -1)
    blocks[0, 4] = shift(blocks[0, -3], 1)
    blocks[1, 4] = shift(blocks[1, 3], -1)

    mine = saturate(query_act)
    other = swap(mine, "core")
    norm, other_norm = normalizer.reshape(4, 128), swap(normalizer, "core").reshape(4, 128)
    at, other_at = positive.reshape(4, 128), swap(positive, "core").reshape(4, 128)
    other, norm, other_norm, at, other_at = lax.optimization_barrier((other, norm, other_norm, at, other_at))

    part, joined = partial_scores(mine, other, [blocks[k] for k in KEYS])
    grad = exchange(score_grad(exchange(part), norm, other_norm, at, other_at))

    joined = after(joined, grad)
    query_grad = query_grads(query_act, grad, swap(grad[4:], "core"), joined, swap(joined, "core"))

    terms = passage_sums(grad, mine, other, 0, [])
    terms.update(passage_sums(grad, mine, other, 256, []))
    both = {d: jnp.concatenate([terms[0, d], terms[1, d]], axis=0) for d in ORDER}
    pad = jnp.zeros((32, 2048), F32)
    up = jnp.concatenate([shift(terms[0, 4].astype(BF16), 1).astype(F32), pad], axis=0)
    down = jnp.concatenate([pad, shift(terms[1, 4].astype(BF16), -1).astype(F32)], axis=0)
    for d in (3, 2, 1):
        up = shift((both[d] + up).astype(BF16), 1).astype(F32)
        down = shift((both[-d] + down).astype(BF16), -1).astype(F32)
    total = both[0] + up + down
    theirs = swap(total[32:].astype(BF16), "ylo").astype(F32)
    total = after(total[:32], query_grad) + theirs
    passage_grad = (total * slope(passage_act)).astype(BF16)
    return (query_grad, passage_grad)


def solution(mesh):
    split = Mesh(mesh.devices.reshape(2, 8, 2, 2, 4), ("ylo", "z", "core", "yhi", "x"))
    rows, columns = ("ylo", "z", "core"), ("yhi", "x")
    return jax.shard_map(
        shards,
        mesh=split,
        in_specs=(P(rows, columns), P(rows, columns), P(rows), P(rows)),
        out_specs=(P(rows, columns), P(rows, columns)),
        check_vma=False,
    )
```

```python
import functools
import math

import jax
import jax.numpy as jnp
from jax import lax
from jax.experimental import pallas as pl
from jax.experimental.pallas import tpu as pltpu
from jax.sharding import Mesh, PartitionSpec as P

VOCAB = 16384
REP = ("x", "yhi")
FACTOR = 8.0 / math.sqrt(VOCAB)
BF16, F32 = jnp.bfloat16, jnp.float32
ORDER = [4, 3, -3, 2, -2, 1, -1, 0]
KEYS = [(s, d) for d in ORDER for s in (0, 1)]
VMEM = pl.BlockSpec(memory_space=pltpu.VMEM)
ANY = pl.BlockSpec(memory_space=pl.ANY)
PARAMS = pltpu.CompilerParams(vmem_limit_bytes=16 * 1024 * 1024)


def shape(dims, dtype):
    return jax.ShapeDtypeStruct(dims, dtype)


def saturate(act):
    wide = jnp.maximum(act.astype(F32), 0.0)
    small = wide - 0.5 * wide * wide
    return jnp.where(wide < 2.0**-8, small, jnp.log(1.0 + wide)).astype(BF16)


def slope(act):
    wide = act.astype(F32)
    return jnp.where(wide > 0.0, 1.0 / (1.0 + jnp.maximum(wide, 0.0)), 0.0)


def swap(value, axis):
    return lax.ppermute(value, axis, [(0, 1), (1, 0)])


def shift(value, step):
    return lax.ppermute(value, "z", [(i, (i + step) % 8) for i in range(8)])


def exchange(value):
    return lax.all_to_all(value, REP, split_axis=0, concat_axis=0)


def after(value, *others):
    return lax.optimization_barrier((value, *others))[0]


def score_kernel(mine_ref, other_ref, *refs):
    blocks, out_ref, joined_ref = refs[:16], refs[-2], refs[-1]
    for i in range(16):
        joined_ref[i * 32 : i * 32 + 32, :] = blocks[i][...]
    for i, ref in enumerate((mine_ref, other_ref)):
        for k in range(2):
            part = lax.dot_general(
                joined_ref[...],
                ref[k * 256 : k * 256 + 256, :],
                (((1,), (1,)), ((), ())),
                preferred_element_type=F32,
            )
            most, least = jnp.max(part, axis=0, keepdims=True), jnp.min(part, axis=0, keepdims=True)
            halves = jnp.round(most + least)
            centre = halves * 0.5
            reach = jnp.maximum(most - centre, centre - least)
            step = jnp.maximum(jnp.ceil(reach * (2.0**17 / 32767)), 1.0)
            code = jnp.round((part - centre) * (2.0**17 / step))
            row = lax.broadcasted_iota(jnp.int32, (16, 256), 0)
            extra = jnp.where(row == 0, halves, jnp.where(row == 1, step, 0.0))
            for n in range(2):
                columns = slice(n * 128, n * 128 + 128)
                at = i * 4 + k * 2 + n
                out_ref[at, :512, :] = code[:, columns].astype(jnp.int32).astype(jnp.int16)
                out_ref[at, 512:, :] = extra[:, columns].astype(jnp.int32).astype(jnp.int16)


def partial_scores(mine, other, blocks):
    return pl.pallas_call(
        score_kernel,
        out_shape=(shape((8, 528, 128), jnp.int16), shape((512, 2048), BF16)),
        in_specs=[VMEM] * 18,
        out_specs=(VMEM, VMEM),
        compiler_params=PARAMS,
    )(mine, other, *blocks)


def grad_kernel(pieces_ref, norm_ref, other_norm_ref, at_ref, other_at_ref, out_ref):
    core, y, z = lax.axis_index("core"), lax.axis_index("ylo"), lax.axis_index("z")
    rep = lax.axis_index("x") * 2 + lax.axis_index("yhi")
    norm = jnp.where(rep < 4, norm_ref[...], other_norm_ref[...])
    positive = jnp.where(rep < 4, at_ref[...], other_at_ref[...])
    turn = lax.broadcasted_iota(jnp.int32, (4, 128), 0) == lax.rem(rep, 4)
    norm = jnp.sum(jnp.where(turn, norm, 0.0), axis=0, keepdims=True)
    positive = jnp.sum(jnp.where(turn, positive, 0), axis=0, keepdims=True)
    scores = 0.0
    for k in range(8):
        extra = pieces_ref[k, 512:, :].astype(jnp.int32).astype(F32)
        code = pieces_ref[k, :512, :].astype(jnp.int32).astype(F32)
        scores = scores + (code * (extra[1:2] * 2.0**-17) + extra[0:1] * 0.5)
    place = lax.broadcasted_iota(jnp.int32, (512, 128), 0)
    turn = place >> 6
    ahead = jnp.where((turn & 1) == 0, 4 + (turn >> 1), (7 - turn) >> 1)
    ident = ((y + (place >> 5)) & 1) * 512 + ((z + ahead) & 7) * 64 + core * 32 + (place & 31)
    onehot = (positive == ident).astype(F32)
    grad = (jnp.exp(scores * FACTOR - norm) - onehot) * (8.0 * FACTOR)
    grad = grad.astype(BF16)
    for k in range(8):
        out_ref[k] = grad


def score_grad(pieces, *rows):
    return pl.pallas_call(
        grad_kernel,
        out_shape=shape((8, 512, 128), BF16),
        in_specs=[VMEM] * 5,
        out_specs=VMEM,
        compiler_params=PARAMS,
    )(pieces, *rows)


def sum_kernel(at, sends, grad_ref, mine_ref, other_ref, *refs):
    out_ref, send_refs = refs[-1 - len(sends)], refs[len(refs) - len(sends) :]
    left = jnp.concatenate([grad_ref[k, at : at + 256, :] for k in range(8)], axis=1)
    for j in range(4):
        columns = slice(j * 512, j * 512 + 512)
        total = jnp.dot(left[:, :512], mine_ref[:, columns], preferred_element_type=F32)
        total += jnp.dot(left[:, 512:], other_ref[:, columns], preferred_element_type=F32)
        out_ref[:, :, columns] = total.reshape(8, 32, 512)
        for i, ref in zip(sends, send_refs):
            ref[:, columns] = total[i * 32 : i * 32 + 32].astype(BF16)


def passage_sums(grad, mine, other, at, sends):
    return pl.pallas_call(
        functools.partial(sum_kernel, at, sends),
        out_shape=(shape((8, 32, 2048), F32),) + (shape((32, 2048), BF16),) * len(sends),
        in_specs=[VMEM] * 3,
        out_specs=(VMEM,) * (1 + len(sends)),
        compiler_params=PARAMS,
    )(grad, mine, other)


def add_kernel(places, *refs):
    n = len(places)
    for i, place in enumerate(places):
        total = refs[2 * i][place] + refs[2 * i + 1][...].astype(F32)
        refs[2 * n + i][...] = total.astype(BF16)


def add_blocks(*items):
    return pl.pallas_call(
        functools.partial(add_kernel, [place for _, place, _ in items]),
        out_shape=(shape((32, 2048), BF16),) * len(items),
        in_specs=[VMEM] * (2 * len(items)),
        out_specs=(VMEM,) * len(items),
        compiler_params=PARAMS,
    )(*[a for sums, _, come in items for a in (sums, come)])


def query_kernel(first, act_ref, own_grad_ref, other_grad_ref, own_ref, other_ref, *refs):
    out_ref, turned_ref = refs[-2:]
    j = pl.program_id(0)

    @pl.when(j == 0)
    def _():
        for i, g in enumerate((own_grad_ref, other_grad_ref)):
            for k in range(4):
                turned_ref[k * 128 : k * 128 + 128, i * 512 : i * 512 + 512] = g[k].T

    columns = pl.ds(pl.multiple_of((j + first) * 512, 512), 512)
    total = jnp.dot(turned_ref[:, :512], own_ref[:, columns], preferred_element_type=F32)
    total += jnp.dot(turned_ref[:, 512:], other_ref[:, columns], preferred_element_type=F32)
    wide = act_ref[...].astype(F32)
    below = 1.0 + jnp.maximum(wide, 0.0)
    guess = pl.reciprocal(below, approx=True)
    inverse = guess * (2.0 - below * guess)
    out_ref[...] = jnp.where(wide > 0.0, total * inverse, 0.0).astype(BF16)


def query_grads(act, grad, other_grad, own, other, begun=None):
    first = 0 if begun is None else 2
    column = pl.BlockSpec((512, 512), lambda j: (0, j + first))
    rest = () if begun is None else (begun,)
    return pl.pallas_call(
        functools.partial(query_kernel, first),
        out_shape=shape((512, 2048), BF16),
        grid=(2,),
        in_specs=[column] + [VMEM] * 4 + [ANY] * len(rest),
        out_specs=column,
        scratch_shapes=[pltpu.VMEM((512, 1024), BF16)],
        input_output_aliases={5: 0} if rest else {},
        compiler_params=PARAMS,
    )(act, grad, other_grad, own, other, *rest)


def shards(query_act, passage_act, positive, normalizer):
    own = saturate(passage_act)
    blocks = {(0, 0): own, (1, 0): swap(own, "ylo")}
    for d in range(1, 4):
        for s in (0, 1):
            blocks[s, -d] = shift(blocks[s, 1 - d], 1)
            blocks[s, d] = shift(blocks[s, d - 1], -1)
    blocks[0, 4] = shift(blocks[0, -3], 1)
    blocks[1, 4] = shift(blocks[1, 3], -1)

    mine = saturate(query_act)
    other = swap(mine, "core")
    norm, other_norm = normalizer.reshape(4, 128), swap(normalizer, "core").reshape(4, 128)
    at, other_at = positive.reshape(4, 128), swap(positive, "core").reshape(4, 128)
    other, norm, other_norm, at, other_at = lax.optimization_barrier((other, norm, other_norm, at, other_at))

    part, joined = partial_scores(mine, other, [blocks[k] for k in KEYS])
    grad = exchange(score_grad(exchange(part), norm, other_norm, at, other_at))

    joined = after(joined, grad)
    query_args = (query_act, grad, swap(grad[4:], "core"), joined, swap(joined, "core"))
    query_begun = query_grads(*query_args)

    far, a0, a1, b0, b1 = passage_sums(grad, mine, other, 0, [0, 1, 4, 3])
    (near,) = passage_sums(grad, mine, other, 256, [])
    place = {k: (far, i) if i < 8 else (near, i - 8) for i, k in enumerate(KEYS)}
    a0, a1, b0, b1 = shift(a0, 1), shift(a1, -1), shift(b0, -1), shift(b1, 1)
    for d in (3, 2, 1):
        a0, a1 = add_blocks((*place[0, d], a0), (*place[1, -d], a1))
        a0, a1 = shift(a0, 1), shift(a1, -1)
        if d > 1:
            b0, b1 = add_blocks((*place[0, 1 - d], b0), (*place[1, d - 1], b1))
            b0, b1 = shift(b0, -1), shift(b1, 1)
    sums = [near[place[s, 0][1]] for s in (0, 1)]
    theirs = after(sums[1], query_begun) + a1.astype(F32) + b1.astype(F32)
    theirs = swap(theirs.astype(BF16), "ylo").astype(F32)
    query_grad = query_grads(*query_args, query_begun)
    total = after(sums[0], query_grad) + a0.astype(F32) + b0.astype(F32) + theirs
    passage_grad = (total * slope(passage_act)).astype(BF16)
    return (query_grad, passage_grad)


def solution(mesh):
    split = Mesh(mesh.devices.reshape(2, 8, 2, 2, 4), ("ylo", "z", "core", "yhi", "x"))
    rows, columns = ("ylo", "z", "core"), ("yhi", "x")
    return jax.shard_map(
        shards,
        mesh=split,
        in_specs=(P(rows, columns), P(rows, columns), P(rows), P(rows)),
        out_specs=(P(rows, columns), P(rows, columns)),
        check_vma=False,
    )
```

```python
import functools
import math

import jax
import jax.numpy as jnp
from jax import lax
from jax.experimental import pallas as pl
from jax.experimental.pallas import tpu as pltpu
from jax.sharding import Mesh, PartitionSpec as P

VOCAB = 16384
REP = ("x", "yhi")
FACTOR = 8.0 / math.sqrt(VOCAB)
BF16, F32 = jnp.bfloat16, jnp.float32
ORDER = [4, 3, -3, 2, -2, 1, -1, 0]
KEYS = [(s, d) for d in ORDER for s in (0, 1)]
LATE = 6
VMEM = pl.BlockSpec(memory_space=pltpu.VMEM)
ANY = pl.BlockSpec(memory_space=pl.ANY)
PARAMS = pltpu.CompilerParams(vmem_limit_bytes=16 * 1024 * 1024)


def shape(dims, dtype):
    return jax.ShapeDtypeStruct(dims, dtype)


def saturate(act):
    wide = jnp.maximum(act.astype(F32), 0.0)
    small = wide - 0.5 * wide * wide
    return jnp.where(wide < 2.0**-8, small, jnp.log(1.0 + wide)).astype(BF16)


def slope(act):
    wide = act.astype(F32)
    return jnp.where(wide > 0.0, 1.0 / (1.0 + jnp.maximum(wide, 0.0)), 0.0)


def swap(value, axis):
    return lax.ppermute(value, axis, [(0, 1), (1, 0)])


def even(value):
    return lax.ppermute(value, "z", [(i, i ^ 1) for i in range(8)])


def odd(value):
    return lax.ppermute(value, "z", [(i, ((i - 1) ^ 1) + 1 & 7) for i in range(8)])


def exchange(value):
    return lax.all_to_all(value, REP, split_axis=0, concat_axis=0)


def after(value, *others):
    return lax.optimization_barrier((value, *others))[0]


def early_kernel(mine_ref, other_ref, *refs):
    *blocks, part_ref, joined_ref = refs
    for i, block in enumerate(blocks):
        joined_ref[LATE * 32 + i * 32 : LATE * 32 + i * 32 + 32, :] = block[...]
    for i, ref in enumerate((mine_ref, other_ref)):
        for k in range(2):
            part_ref[i * 2 + k] = lax.dot_general(
                joined_ref[LATE * 32 :, :],
                ref[k * 256 : k * 256 + 256, :],
                (((1,), (1,)), ((), ())),
                preferred_element_type=F32,
            )


def score_kernel(mine_ref, other_ref, early_ref, _, *refs):
    *blocks, out_ref, joined_ref = refs
    for i, block in enumerate(blocks):
        joined_ref[i * 32 : i * 32 + 32, :] = block[...]
    for i, ref in enumerate((mine_ref, other_ref)):
        for k in range(2):
            early = early_ref[i * 2 + k]
            late = lax.dot_general(
                joined_ref[...],
                ref[k * 256 : k * 256 + 256, :],
                (((1,), (1,)), ((), ())),
                preferred_element_type=F32,
            )
            most = jnp.maximum(jnp.max(early, axis=0, keepdims=True), jnp.max(late, axis=0, keepdims=True))
            least = jnp.minimum(jnp.min(early, axis=0, keepdims=True), jnp.min(late, axis=0, keepdims=True))
            halves = jnp.round(most + least)
            centre = halves * 0.5
            reach = jnp.maximum(most - centre, centre - least)
            step = jnp.maximum(jnp.ceil(reach * (2.0**17 / 32767)), 1.0)
            scale = 2.0**17 / step
            row = lax.broadcasted_iota(jnp.int32, (16, 256), 0)
            extra = jnp.where(row == 0, halves, jnp.where(row == 1, step, 0.0))
            for n in range(2):
                columns = slice(n * 128, n * 128 + 128)
                at = i * 4 + k * 2 + n
                for start, part in ((0, late), (LATE * 32, early)):
                    code = jnp.round((part[:, columns] - centre[:, columns]) * scale[:, columns])
                    out_ref[at, start : start + part.shape[0], :] = code.astype(jnp.int32).astype(jnp.int16)
                out_ref[at, 512:, :] = extra[:, columns].astype(jnp.int32).astype(jnp.int16)


def partial_scores(mine, other, blocks):
    early, joined = pl.pallas_call(
        early_kernel,
        out_shape=(shape((4, 512 - LATE * 32, 256), F32), shape((512, 2048), BF16)),
        in_specs=[VMEM] * (18 - LATE),
        out_specs=(VMEM, VMEM),
        compiler_params=PARAMS,
    )(mine, other, *blocks[LATE:])
    return pl.pallas_call(
        score_kernel,
        out_shape=(shape((8, 528, 128), jnp.int16), shape((512, 2048), BF16)),
        grid=(1,),
        in_specs=[VMEM] * 3 + [ANY] + [VMEM] * LATE,
        out_specs=(VMEM, pl.BlockSpec((LATE * 32, 2048), lambda j: (0, 0))),
        input_output_aliases={3: 1},
        compiler_params=PARAMS,
    )(mine, other, early, joined, *blocks[:LATE])


def grad_kernel(pieces_ref, norm_ref, other_norm_ref, at_ref, other_at_ref, out_ref):
    core, y, z = lax.axis_index("core"), lax.axis_index("ylo"), lax.axis_index("z")
    rep = lax.axis_index("x") * 2 + lax.axis_index("yhi")
    norm = jnp.where(rep < 4, norm_ref[...], other_norm_ref[...])
    positive = jnp.where(rep < 4, at_ref[...], other_at_ref[...])
    turn = lax.broadcasted_iota(jnp.int32, (4, 128), 0) == lax.rem(rep, 4)
    norm = jnp.sum(jnp.where(turn, norm, 0.0), axis=0, keepdims=True)
    positive = jnp.sum(jnp.where(turn, positive, 0), axis=0, keepdims=True)
    scores = 0.0
    for k in range(8):
        extra = pieces_ref[k, 512:, :].astype(jnp.int32).astype(F32)
        code = pieces_ref[k, :512, :].astype(jnp.int32).astype(F32)
        scores = scores + (code * (extra[1:2] * 2.0**-17) + extra[0:1] * 0.5)
    place = lax.broadcasted_iota(jnp.int32, (512, 128), 0)
    turn = place >> 6
    ahead = jnp.where((turn & 1) == 0, 4 + (turn >> 1), (7 - turn) >> 1)
    ahead = jnp.where((z & 1) == 0, ahead, 8 - ahead)
    ident = ((y + (place >> 5)) & 1) * 512 + ((z + ahead) & 7) * 64 + core * 32 + (place & 31)
    onehot = (positive == ident).astype(F32)
    grad = (jnp.exp(scores * FACTOR - norm) - onehot) * (8.0 * FACTOR)
    grad = grad.astype(BF16)
    for k in range(8):
        out_ref[k] = grad


def score_grad(pieces, *rows):
    return pl.pallas_call(
        grad_kernel,
        out_shape=shape((8, 512, 128), BF16),
        in_specs=[VMEM] * 5,
        out_specs=VMEM,
        compiler_params=PARAMS,
    )(pieces, *rows)


def sum_kernel(at, sends, grad_ref, mine_ref, other_ref, *refs):
    out_ref, send_refs = refs[-1 - len(sends)], refs[len(refs) - len(sends) :]
    left = jnp.concatenate([grad_ref[k, at : at + 256, :] for k in range(8)], axis=1)
    for j in range(4):
        columns = slice(j * 512, j * 512 + 512)
        total = jnp.dot(left[:, :512], mine_ref[:, columns], preferred_element_type=F32)
        total += jnp.dot(left[:, 512:], other_ref[:, columns], preferred_element_type=F32)
        out_ref[:, :, columns] = total.reshape(8, 32, 512)
        for i, ref in zip(sends, send_refs):
            ref[:, columns] = total[i * 32 : i * 32 + 32].astype(BF16)


def passage_sums(grad, mine, other, at, sends):
    return pl.pallas_call(
        functools.partial(sum_kernel, at, sends),
        out_shape=(shape((8, 32, 2048), F32),) + (shape((32, 2048), BF16),) * len(sends),
        in_specs=[VMEM] * 3,
        out_specs=(VMEM,) * (1 + len(sends)),
        compiler_params=PARAMS,
    )(grad, mine, other)


def add_kernel(items, *refs):
    outs = refs[len(refs) - len(items) :]
    at = 0
    for (place, n), out in zip(items, outs):
        total = refs[at][place]
        for come in refs[at + 1 : at + 1 + n]:
            total = total + come[...].astype(F32)
        out[...] = total.astype(BF16)
        at += 1 + n


def add_blocks(*items):
    return pl.pallas_call(
        functools.partial(add_kernel, [(place, len(come)) for _, place, *come in items]),
        out_shape=(shape((32, 2048), BF16),) * len(items),
        in_specs=[VMEM] * sum(len(item) - 1 for item in items),
        out_specs=(VMEM,) * len(items),
        compiler_params=PARAMS,
    )(*[a for sums, _, *come in items for a in (sums, *come)])


def query_kernel(first, act_ref, own_grad_ref, other_grad_ref, own_ref, other_ref, *refs):
    out_ref, turned_ref = refs[-2:]
    j = pl.program_id(0)

    @pl.when(j == 0)
    def _():
        for i, g in enumerate((own_grad_ref, other_grad_ref)):
            for k in range(4):
                turned_ref[k * 128 : k * 128 + 128, i * 512 : i * 512 + 512] = g[k].T

    columns = pl.ds(pl.multiple_of((j + first) * 512, 512), 512)
    total = jnp.dot(turned_ref[:, :512], own_ref[:, columns], preferred_element_type=F32)
    total += jnp.dot(turned_ref[:, 512:], other_ref[:, columns], preferred_element_type=F32)
    wide = act_ref[...].astype(F32)
    below = 1.0 + jnp.maximum(wide, 0.0)
    guess = pl.reciprocal(below, approx=True)
    inverse = guess * (2.0 - below * guess)
    out_ref[...] = jnp.where(wide > 0.0, total * inverse, 0.0).astype(BF16)


def query_grads(act, grad, other_grad, own, other, begun=None):
    first = 0 if begun is None else 2
    column = pl.BlockSpec((512, 512), lambda j: (0, j + first))
    rest = () if begun is None else (begun,)
    return pl.pallas_call(
        functools.partial(query_kernel, first),
        out_shape=shape((512, 2048), BF16),
        grid=(2,),
        in_specs=[column] + [VMEM] * 4 + [ANY] * len(rest),
        out_specs=column,
        scratch_shapes=[pltpu.VMEM((512, 1024), BF16)],
        input_output_aliases={5: 0} if rest else {},
        compiler_params=PARAMS,
    )(act, grad, other_grad, own, other, *rest)


def shards(query_act, passage_act, positive, normalizer):
    own = saturate(passage_act)
    blocks = {(0, 0): own, (1, 0): swap(own, "ylo")}
    for d in range(1, 4):
        for s in (0, 1):
            blocks[s, d], blocks[s, -d] = even(blocks[s, 1 - d]), odd(blocks[s, d - 1])
    blocks[0, 4], blocks[1, 4] = even(blocks[0, -3]), odd(blocks[1, 3])

    mine = saturate(query_act)
    other = swap(mine, "core")
    norm, other_norm = normalizer.reshape(4, 128), swap(normalizer, "core").reshape(4, 128)
    at, other_at = positive.reshape(4, 128), swap(positive, "core").reshape(4, 128)
    blocks[0, 4], norm, other_norm, at, other_at = lax.optimization_barrier(
        (blocks[0, 4], norm, other_norm, at, other_at)
    )

    part, joined = partial_scores(mine, other, [blocks[k] for k in KEYS])
    grad = exchange(score_grad(exchange(part), norm, other_norm, at, other_at))

    joined = after(joined, grad)
    query_args = (query_act, grad, swap(grad[4:], "core"), joined, swap(joined, "core"))
    query_begun = query_grads(*query_args)

    far, a0, a1, b0, b1 = passage_sums(grad, mine, other, 0, [0, 1, 2, 5])
    (near,) = passage_sums(grad, mine, other, 256, [])
    place = {k: (far, i) if i < 8 else (near, i - 8) for i, k in enumerate(KEYS)}
    a0, a1, b0, b1 = even(a0), odd(a1), even(b0), odd(b1)
    for d in (-3, 2, -1):
        ways = (odd, even) if d < 0 else (even, odd)
        a0, a1 = add_blocks((*place[0, d], a0), (*place[1, -d], a1))
        a0, a1 = ways[0](a0), ways[1](a1)
        if d != -1:
            d = -2 if d < 0 else 1
            b0, b1 = add_blocks((*place[0, d], b0), (*place[1, -d], b1))
            b0, b1 = ways[0](b0), ways[1](b1)
    sums = [near[place[s, 0][1]] for s in (0, 1)]
    theirs = after(sums[1], query_begun) + a1.astype(F32) + b1.astype(F32)
    theirs = swap(theirs.astype(BF16), "ylo").astype(F32)
    query_grad = query_grads(*query_args, query_begun)
    total = after(sums[0], query_grad) + a0.astype(F32) + b0.astype(F32) + theirs
    passage_grad = (total * slope(passage_act)).astype(BF16)
    return (query_grad, passage_grad)


def solution(mesh):
    split = Mesh(mesh.devices.reshape(2, 8, 2, 2, 4), ("ylo", "z", "core", "yhi", "x"))
    rows, columns = ("ylo", "z", "core"), ("yhi", "x")
    return jax.shard_map(
        shards,
        mesh=split,
        in_specs=(P(rows, columns), P(rows, columns), P(rows), P(rows)),
        out_specs=(P(rows, columns), P(rows, columns)),
        check_vma=False,
    )
```

```python
import functools
import math

import jax
import jax.numpy as jnp
from jax import lax
from jax.experimental import pallas as pl
from jax.experimental.pallas import tpu as pltpu
from jax.sharding import Mesh, PartitionSpec as P

VOCAB = 16384
REP = ("x", "yhi")
FACTOR = 8.0 / math.sqrt(VOCAB)
BF16, F32 = jnp.bfloat16, jnp.float32
ORDER = [4, 3, -3, 2, -2, 1, -1, 0]
KEYS = [(s, d) for d in ORDER for s in (0, 1)]
LATE = 6
VMEM = pl.BlockSpec(memory_space=pltpu.VMEM)
ANY = pl.BlockSpec(memory_space=pl.ANY)
PARAMS = pltpu.CompilerParams(vmem_limit_bytes=16 * 1024 * 1024)


def shape(dims, dtype):
    return jax.ShapeDtypeStruct(dims, dtype)


def saturate(act):
    wide = jnp.maximum(act.astype(F32), 0.0)
    small = wide - 0.5 * wide * wide
    return jnp.where(wide < 2.0**-8, small, jnp.log(1.0 + wide)).astype(BF16)


def slope(act):
    wide = act.astype(F32)
    return jnp.where(wide > 0.0, 1.0 / (1.0 + jnp.maximum(wide, 0.0)), 0.0)


def swap(value, axis):
    return lax.ppermute(value, axis, [(0, 1), (1, 0)])


def even(value):
    return lax.ppermute(value, "z", [(i, i ^ 1) for i in range(8)])


def odd(value):
    return lax.ppermute(value, "z", [(i, ((i - 1) ^ 1) + 1 & 7) for i in range(8)])


def cross(value, way):
    to = [i ^ 1 if way is even else ((i - 1) ^ 1) + 1 & 7 for i in range(8)]
    return lax.ppermute(value, ("ylo", "z"), [(y * 8 + i, (1 - y) * 8 + to[i]) for y in (0, 1) for i in range(8)])


def exchange(value):
    return lax.all_to_all(value, REP, split_axis=0, concat_axis=0)


def after(value, *others):
    return lax.optimization_barrier((value, *others))[0]


def early_kernel(mine_ref, other_ref, *refs):
    *blocks, part_ref, joined_ref = refs
    for i, block in enumerate(blocks):
        joined_ref[LATE * 32 + i * 32 : LATE * 32 + i * 32 + 32, :] = block[...]
    for i, ref in enumerate((mine_ref, other_ref)):
        for k in range(2):
            part_ref[i * 2 + k] = lax.dot_general(
                joined_ref[LATE * 32 :, :],
                ref[k * 256 : k * 256 + 256, :],
                (((1,), (1,)), ((), ())),
                preferred_element_type=F32,
            )


def score_kernel(mine_ref, other_ref, early_ref, _, *refs):
    *blocks, out_ref, joined_ref = refs
    for i, block in enumerate(blocks):
        joined_ref[i * 32 : i * 32 + 32, :] = block[...]
    for i, ref in enumerate((mine_ref, other_ref)):
        for k in range(2):
            early = early_ref[i * 2 + k]
            late = lax.dot_general(
                joined_ref[...],
                ref[k * 256 : k * 256 + 256, :],
                (((1,), (1,)), ((), ())),
                preferred_element_type=F32,
            )
            most = jnp.maximum(jnp.max(early, axis=0, keepdims=True), jnp.max(late, axis=0, keepdims=True))
            least = jnp.minimum(jnp.min(early, axis=0, keepdims=True), jnp.min(late, axis=0, keepdims=True))
            halves = jnp.round(most + least)
            centre = halves * 0.5
            reach = jnp.maximum(most - centre, centre - least)
            step = jnp.maximum(jnp.ceil(reach * (2.0**17 / 32767)), 1.0)
            scale = 2.0**17 / step
            row = lax.broadcasted_iota(jnp.int32, (16, 256), 0)
            extra = jnp.where(row == 0, halves, jnp.where(row == 1, step, 0.0))
            for n in range(2):
                columns = slice(n * 128, n * 128 + 128)
                at = i * 4 + k * 2 + n
                for start, part in ((0, late), (LATE * 32, early)):
                    code = jnp.round((part[:, columns] - centre[:, columns]) * scale[:, columns])
                    out_ref[at, start : start + part.shape[0], :] = code.astype(jnp.int32).astype(jnp.int16)
                out_ref[at, 512:, :] = extra[:, columns].astype(jnp.int32).astype(jnp.int16)


def partial_scores(mine, other, blocks):
    early, joined = pl.pallas_call(
        early_kernel,
        out_shape=(shape((4, 512 - LATE * 32, 256), F32), shape((512, 2048), BF16)),
        in_specs=[VMEM] * (18 - LATE),
        out_specs=(VMEM, VMEM),
        compiler_params=PARAMS,
    )(mine, other, *blocks[LATE:])
    return pl.pallas_call(
        score_kernel,
        out_shape=(shape((8, 528, 128), jnp.int16), shape((512, 2048), BF16)),
        grid=(1,),
        in_specs=[VMEM] * 3 + [ANY] + [VMEM] * LATE,
        out_specs=(VMEM, pl.BlockSpec((LATE * 32, 2048), lambda j: (0, 0))),
        input_output_aliases={3: 1},
        compiler_params=PARAMS,
    )(mine, other, early, joined, *blocks[:LATE])


def grad_kernel(pieces_ref, norm_ref, other_norm_ref, at_ref, other_at_ref, out_ref):
    core, y, z = lax.axis_index("core"), lax.axis_index("ylo"), lax.axis_index("z")
    rep = lax.axis_index("x") * 2 + lax.axis_index("yhi")
    norm = jnp.where(rep < 4, norm_ref[...], other_norm_ref[...])
    positive = jnp.where(rep < 4, at_ref[...], other_at_ref[...])
    turn = lax.broadcasted_iota(jnp.int32, (4, 128), 0) == lax.rem(rep, 4)
    norm = jnp.sum(jnp.where(turn, norm, 0.0), axis=0, keepdims=True)
    positive = jnp.sum(jnp.where(turn, positive, 0), axis=0, keepdims=True)
    scores = 0.0
    for k in range(8):
        extra = pieces_ref[k, 512:, :].astype(jnp.int32).astype(F32)
        code = pieces_ref[k, :512, :].astype(jnp.int32).astype(F32)
        scores = scores + (code * (extra[1:2] * 2.0**-17) + extra[0:1] * 0.5)
    place = lax.broadcasted_iota(jnp.int32, (512, 128), 0)
    turn = place >> 6
    ahead = jnp.where((turn & 1) == 0, 4 + (turn >> 1), (7 - turn) >> 1)
    ahead = jnp.where((z & 1) == 0, ahead, 8 - ahead)
    ident = ((y + (place >> 5)) & 1) * 512 + ((z + ahead) & 7) * 64 + core * 32 + (place & 31)
    onehot = (positive == ident).astype(F32)
    grad = (jnp.exp(scores * FACTOR - norm) - onehot) * (8.0 * FACTOR)
    grad = grad.astype(BF16)
    for k in range(8):
        out_ref[k] = grad


def score_grad(pieces, *rows):
    return pl.pallas_call(
        grad_kernel,
        out_shape=shape((8, 512, 128), BF16),
        in_specs=[VMEM] * 5,
        out_specs=VMEM,
        compiler_params=PARAMS,
    )(pieces, *rows)


def sum_kernel(at, sends, grad_ref, mine_ref, other_ref, *refs):
    out_ref, send_refs = refs[-1 - len(sends)], refs[len(refs) - len(sends) :]
    left = jnp.concatenate([grad_ref[k, at : at + 256, :] for k in range(8)], axis=1)
    for j in range(4):
        columns = slice(j * 512, j * 512 + 512)
        total = jnp.dot(left[:, :512], mine_ref[:, columns], preferred_element_type=F32)
        total += jnp.dot(left[:, 512:], other_ref[:, columns], preferred_element_type=F32)
        out_ref[:, :, columns] = total.reshape(8, 32, 512)
        for i, ref in zip(sends, send_refs):
            ref[:, columns] = total[i * 32 : i * 32 + 32].astype(BF16)


def passage_sums(grad, mine, other, at, sends):
    return pl.pallas_call(
        functools.partial(sum_kernel, at, sends),
        out_shape=(shape((8, 32, 2048), F32),) + (shape((32, 2048), BF16),) * len(sends),
        in_specs=[VMEM] * 3,
        out_specs=(VMEM,) * (1 + len(sends)),
        compiler_params=PARAMS,
    )(grad, mine, other)


def add_kernel(items, *refs):
    outs = refs[len(refs) - len(items) :]
    at = 0
    for (place, n), out in zip(items, outs):
        total = refs[at][place]
        for come in refs[at + 1 : at + 1 + n]:
            total = total + come[...].astype(F32)
        out[...] = total.astype(BF16)
        at += 1 + n


def add_blocks(*items):
    return pl.pallas_call(
        functools.partial(add_kernel, [(place, len(come)) for _, place, *come in items]),
        out_shape=(shape((32, 2048), BF16),) * len(items),
        in_specs=[VMEM] * sum(len(item) - 1 for item in items),
        out_specs=(VMEM,) * len(items),
        compiler_params=PARAMS,
    )(*[a for sums, _, *come in items for a in (sums, *come)])


def query_kernel(act_ref, own_grad_ref, other_grad_ref, own_ref, other_ref, out_ref, turned_ref):
    for i, g in enumerate((own_grad_ref, other_grad_ref)):
        for k in range(4):
            turned_ref[k * 128 : k * 128 + 128, i * 512 : i * 512 + 512] = g[k].T
    for j in range(4):
        columns = slice(j * 512, j * 512 + 512)
        total = jnp.dot(turned_ref[:, :512], own_ref[:, columns], preferred_element_type=F32)
        total += jnp.dot(turned_ref[:, 512:], other_ref[:, columns], preferred_element_type=F32)
        wide = act_ref[:, columns].astype(F32)
        below = 1.0 + jnp.maximum(wide, 0.0)
        guess = pl.reciprocal(below, approx=True)
        inverse = guess * (2.0 - below * guess)
        out_ref[:, columns] = jnp.where(wide > 0.0, total * inverse, 0.0).astype(BF16)


def query_grads(act, grad, other_grad, own, other):
    return pl.pallas_call(
        query_kernel,
        out_shape=shape((512, 2048), BF16),
        in_specs=[VMEM] * 5,
        out_specs=VMEM,
        scratch_shapes=[pltpu.VMEM((512, 1024), BF16)],
        compiler_params=PARAMS,
    )(act, grad[:4], other_grad, own, other)


def shards(query_act, passage_act, positive, normalizer):
    own = saturate(passage_act)
    blocks = {(0, 0): own, (1, 0): swap(own, "ylo")}
    for d in range(1, 4):
        for s in (0, 1):
            blocks[s, d], blocks[s, -d] = even(blocks[s, 1 - d]), odd(blocks[s, d - 1])
    blocks[0, 4], blocks[1, 4] = even(blocks[0, -3]), odd(blocks[1, 3])

    mine = saturate(query_act)
    other = swap(mine, "core")
    norm, other_norm = normalizer.reshape(4, 128), swap(normalizer, "core").reshape(4, 128)
    at, other_at = positive.reshape(4, 128), swap(positive, "core").reshape(4, 128)
    blocks[0, 4], norm, other_norm, at, other_at = lax.optimization_barrier(
        (blocks[0, 4], norm, other_norm, at, other_at)
    )

    part, joined = partial_scores(mine, other, [blocks[k] for k in KEYS])
    grad = exchange(score_grad(exchange(part), norm, other_norm, at, other_at))

    joined = after(joined, grad)
    query_grad = query_grads(query_act, grad, swap(grad[4:], "core"), joined, swap(joined, "core"))

    far, a0, a1, b0, b1 = passage_sums(grad, mine, other, 0, [0, 1, 2, 5])
    (near,) = passage_sums(grad, mine, other, 256, [])
    place = {k: (far, i) if i < 8 else (near, i - 8) for i, k in enumerate(KEYS)}
    a0, a1, b0, b1 = even(a0), odd(a1), even(b0), odd(b1)
    for d in (-3, 2, -1):
        ways = (odd, even) if d < 0 else (even, odd)
        (a0,), (a1,) = add_blocks((*place[0, d], a0)), add_blocks((*place[1, -d], a1))
        a0, a1 = ways[0](a0), cross(a1, even) if d == -1 else ways[1](a1)
        if d != -1:
            d = -2 if d < 0 else 1
            (b0,), (b1,) = add_blocks((*place[0, d], b0)), add_blocks((*place[1, -d], b1))
            b0, b1 = ways[0](b0), ways[1](b1)
    sums = [near[place[s, 0][1]] for s in (0, 1)]
    theirs = swap((sums[1] + b1.astype(F32)).astype(BF16), "ylo").astype(F32)
    total = after(sums[0], query_grad) + a0.astype(F32) + a1.astype(F32) + b0.astype(F32) + theirs
    passage_grad = (total * slope(passage_act)).astype(BF16)
    return (query_grad, passage_grad)


def solution(mesh):
    split = Mesh(mesh.devices.reshape(2, 8, 2, 2, 4), ("ylo", "z", "core", "yhi", "x"))
    rows, columns = ("ylo", "z", "core"), ("yhi", "x")
    return jax.shard_map(
        shards,
        mesh=split,
        in_specs=(P(rows, columns), P(rows, columns), P(rows), P(rows)),
        out_specs=(P(rows, columns), P(rows, columns)),
        check_vma=False,
    )
```

```python
import functools
import math

import jax
import jax.numpy as jnp
from jax import lax
from jax.experimental import pallas as pl
from jax.experimental.pallas import tpu as pltpu
from jax.sharding import Mesh, PartitionSpec as P

VOCAB = 16384
REP = ("x", "yhi")
FACTOR = 8.0 / math.sqrt(VOCAB)
BF16, F32 = jnp.bfloat16, jnp.float32
ORDER = [4, 3, -3, 2, -2, 1, -1, 0]
KEYS = [(s, d) for d in ORDER for s in (0, 1)]
LATE = 4
VMEM = pl.BlockSpec(memory_space=pltpu.VMEM)
ANY = pl.BlockSpec(memory_space=pl.ANY)
PARAMS = pltpu.CompilerParams(vmem_limit_bytes=16 * 1024 * 1024)


def shape(dims, dtype):
    return jax.ShapeDtypeStruct(dims, dtype)


def saturate(act):
    wide = jnp.maximum(act.astype(F32), 0.0)
    small = wide - 0.5 * wide * wide
    return jnp.where(wide < 2.0**-8, small, jnp.log(1.0 + wide)).astype(BF16)


def slope(act):
    wide = act.astype(F32)
    return jnp.where(wide > 0.0, 1.0 / (1.0 + jnp.maximum(wide, 0.0)), 0.0)


def swap(value, axis):
    return lax.ppermute(value, axis, [(0, 1), (1, 0)])


def even(value):
    return lax.ppermute(value, "z", [(i, i ^ 1) for i in range(8)])


def odd(value):
    return lax.ppermute(value, "z", [(i, ((i - 1) ^ 1) + 1 & 7) for i in range(8)])


def cross(value, way):
    to = [i ^ 1 if way is even else ((i - 1) ^ 1) + 1 & 7 for i in range(8)]
    return lax.ppermute(value, ("ylo", "z"), [(y * 8 + i, (1 - y) * 8 + to[i]) for y in (0, 1) for i in range(8)])


def exchange(value):
    return lax.all_to_all(value, REP, split_axis=0, concat_axis=0)


def after(value, *others):
    return lax.optimization_barrier((value, *others))[0]


def early_kernel(mine_ref, other_ref, *refs):
    *blocks, part_ref, joined_ref = refs
    for i, block in enumerate(blocks):
        joined_ref[LATE * 32 + i * 32 : LATE * 32 + i * 32 + 32, :] = block[...]
    for i, ref in enumerate((mine_ref, other_ref)):
        for k in range(2):
            part_ref[i * 2 + k] = lax.dot_general(
                joined_ref[LATE * 32 :, :],
                ref[k * 256 : k * 256 + 256, :],
                (((1,), (1,)), ((), ())),
                preferred_element_type=F32,
            )


def score_kernel(mine_ref, other_ref, early_ref, _, *refs):
    *blocks, out_ref, joined_ref = refs
    for i, block in enumerate(blocks):
        joined_ref[i * 32 : i * 32 + 32, :] = block[...]
    for i, ref in enumerate((mine_ref, other_ref)):
        for k in range(2):
            early = early_ref[i * 2 + k]
            late = lax.dot_general(
                joined_ref[...],
                ref[k * 256 : k * 256 + 256, :],
                (((1,), (1,)), ((), ())),
                preferred_element_type=F32,
            )
            most = jnp.maximum(jnp.max(early, axis=0, keepdims=True), jnp.max(late, axis=0, keepdims=True))
            least = jnp.minimum(jnp.min(early, axis=0, keepdims=True), jnp.min(late, axis=0, keepdims=True))
            halves = jnp.round(most + least)
            centre = halves * 0.5
            reach = jnp.maximum(most - centre, centre - least)
            step = jnp.maximum(jnp.ceil(reach * (2.0**17 / 32767)), 1.0)
            scale = 2.0**17 / step
            row = lax.broadcasted_iota(jnp.int32, (16, 256), 0)
            extra = jnp.where(row == 0, halves, jnp.where(row == 1, step, 0.0))
            for n in range(2):
                columns = slice(n * 128, n * 128 + 128)
                at = i * 4 + k * 2 + n
                for start, part in ((0, late), (LATE * 32, early)):
                    code = jnp.round((part[:, columns] - centre[:, columns]) * scale[:, columns])
                    out_ref[at, start : start + part.shape[0], :] = code.astype(jnp.int32).astype(jnp.int16)
                out_ref[at, 512:, :] = extra[:, columns].astype(jnp.int32).astype(jnp.int16)


def partial_scores(mine, other, blocks):
    early, joined = pl.pallas_call(
        early_kernel,
        out_shape=(shape((4, 512 - LATE * 32, 256), F32), shape((512, 2048), BF16)),
        in_specs=[VMEM] * (18 - LATE),
        out_specs=(VMEM, VMEM),
        compiler_params=PARAMS,
    )(mine, other, *blocks[LATE:])
    return pl.pallas_call(
        score_kernel,
        out_shape=(shape((8, 528, 128), jnp.int16), shape((512, 2048), BF16)),
        grid=(1,),
        in_specs=[VMEM] * 3 + [ANY] + [VMEM] * LATE,
        out_specs=(VMEM, pl.BlockSpec((LATE * 32, 2048), lambda j: (0, 0))),
        input_output_aliases={3: 1},
        compiler_params=PARAMS,
    )(mine, other, early, joined, *blocks[:LATE])


def grad_kernel(pieces_ref, norm_ref, other_norm_ref, at_ref, other_at_ref, out_ref):
    core, y, z = lax.axis_index("core"), lax.axis_index("ylo"), lax.axis_index("z")
    rep = lax.axis_index("x") * 2 + lax.axis_index("yhi")
    norm = jnp.where(rep < 4, norm_ref[...], other_norm_ref[...])
    positive = jnp.where(rep < 4, at_ref[...], other_at_ref[...])
    turn = lax.broadcasted_iota(jnp.int32, (4, 128), 0) == lax.rem(rep, 4)
    norm = jnp.sum(jnp.where(turn, norm, 0.0), axis=0, keepdims=True)
    positive = jnp.sum(jnp.where(turn, positive, 0), axis=0, keepdims=True)
    scores = 0.0
    for k in range(8):
        extra = pieces_ref[k, 512:, :].astype(jnp.int32).astype(F32)
        code = pieces_ref[k, :512, :].astype(jnp.int32).astype(F32)
        scores = scores + (code * (extra[1:2] * 2.0**-17) + extra[0:1] * 0.5)
    place = lax.broadcasted_iota(jnp.int32, (512, 128), 0)
    turn = place >> 6
    ahead = jnp.where((turn & 1) == 0, 4 + (turn >> 1), (7 - turn) >> 1)
    ahead = jnp.where((z & 1) == 0, ahead, 8 - ahead)
    ident = ((y + (place >> 5)) & 1) * 512 + ((z + ahead) & 7) * 64 + core * 32 + (place & 31)
    onehot = (positive == ident).astype(F32)
    grad = (jnp.exp(scores * FACTOR - norm) - onehot) * (8.0 * FACTOR)
    grad = grad.astype(BF16)
    for k in range(8):
        out_ref[k] = grad


def score_grad(pieces, *rows):
    return pl.pallas_call(
        grad_kernel,
        out_shape=shape((8, 512, 128), BF16),
        in_specs=[VMEM] * 5,
        out_specs=VMEM,
        compiler_params=PARAMS,
    )(pieces, *rows)


def sum_kernel(at, sends, grad_ref, mine_ref, other_ref, *refs):
    out_ref, send_refs = refs[-1 - len(sends)], refs[len(refs) - len(sends) :]
    left = jnp.concatenate([grad_ref[k, at : at + 256, :] for k in range(8)], axis=1)
    for j in range(4):
        columns = slice(j * 512, j * 512 + 512)
        total = jnp.dot(left[:, :512], mine_ref[:, columns], preferred_element_type=F32)
        total += jnp.dot(left[:, 512:], other_ref[:, columns], preferred_element_type=F32)
        out_ref[:, :, columns] = total.reshape(8, 32, 512)
        for i, ref in zip(sends, send_refs):
            ref[:, columns] = total[i * 32 : i * 32 + 32].astype(BF16)


def passage_sums(grad, mine, other, at, sends):
    return pl.pallas_call(
        functools.partial(sum_kernel, at, sends),
        out_shape=(shape((8, 32, 2048), F32),) + (shape((32, 2048), BF16),) * len(sends),
        in_specs=[VMEM] * 3,
        out_specs=(VMEM,) * (1 + len(sends)),
        compiler_params=PARAMS,
    )(grad, mine, other)


def add_kernel(items, *refs):
    outs = refs[len(refs) - len(items) :]
    at = 0
    for (place, n), out in zip(items, outs):
        total = refs[at][place]
        for come in refs[at + 1 : at + 1 + n]:
            total = total + come[...].astype(F32)
        out[...] = total.astype(BF16)
        at += 1 + n


def add_blocks(*items):
    return pl.pallas_call(
        functools.partial(add_kernel, [(place, len(come)) for _, place, *come in items]),
        out_shape=(shape((32, 2048), BF16),) * len(items),
        in_specs=[VMEM] * sum(len(item) - 1 for item in items),
        out_specs=(VMEM,) * len(items),
        compiler_params=PARAMS,
    )(*[a for sums, _, *come in items for a in (sums, *come)])


def query_kernel(act_ref, own_grad_ref, other_grad_ref, own_ref, other_ref, out_ref, turned_ref):
    for i, g in enumerate((own_grad_ref, other_grad_ref)):
        for k in range(4):
            turned_ref[k * 128 : k * 128 + 128, i * 512 : i * 512 + 512] = g[k].T
    for j in range(4):
        columns = slice(j * 512, j * 512 + 512)
        total = jnp.dot(turned_ref[:, :512], own_ref[:, columns], preferred_element_type=F32)
        total += jnp.dot(turned_ref[:, 512:], other_ref[:, columns], preferred_element_type=F32)
        wide = act_ref[:, columns].astype(F32)
        below = 1.0 + jnp.maximum(wide, 0.0)
        guess = pl.reciprocal(below, approx=True)
        inverse = guess * (2.0 - below * guess)
        out_ref[:, columns] = jnp.where(wide > 0.0, total * inverse, 0.0).astype(BF16)


def query_grads(act, grad, other_grad, own, other):
    return pl.pallas_call(
        query_kernel,
        out_shape=shape((512, 2048), BF16),
        in_specs=[VMEM] * 5,
        out_specs=VMEM,
        scratch_shapes=[pltpu.VMEM((512, 1024), BF16)],
        compiler_params=PARAMS,
    )(act, grad[:4], other_grad, own, other)


def shards(query_act, passage_act, positive, normalizer):
    own = saturate(passage_act)
    blocks = {(0, 0): own, (1, 0): swap(own, "ylo")}
    for d in range(1, 4):
        for s in (0, 1):
            blocks[s, d], blocks[s, -d] = even(blocks[s, 1 - d]), odd(blocks[s, d - 1])
    blocks[0, 4], blocks[1, 4] = even(blocks[0, -3]), odd(blocks[1, 3])

    mine = saturate(query_act)
    other = swap(mine, "core")
    norm, other_norm = normalizer.reshape(4, 128), swap(normalizer, "core").reshape(4, 128)
    at, other_at = positive.reshape(4, 128), swap(positive, "core").reshape(4, 128)
    blocks[0, 4], norm, other_norm, at, other_at = lax.optimization_barrier(
        (blocks[0, 4], norm, other_norm, at, other_at)
    )

    part, joined = partial_scores(mine, other, [blocks[k] for k in KEYS])
    grad = exchange(score_grad(exchange(part), norm, other_norm, at, other_at))

    joined = after(joined, grad)
    query_grad = query_grads(query_act, grad, swap(grad[4:], "core"), joined, swap(joined, "core"))

    far, a0, a1, b0, b1 = passage_sums(grad, mine, other, 0, [0, 1, 2, 5])
    (near,) = passage_sums(grad, mine, other, 256, [])
    place = {k: (far, i) if i < 8 else (near, i - 8) for i, k in enumerate(KEYS)}
    a0, a1, b0, b1 = even(a0), odd(a1), even(b0), odd(b1)
    for d in (-3, 2, -1):
        ways = (odd, even) if d < 0 else (even, odd)
        (a0,), (a1,) = add_blocks((*place[0, d], a0)), add_blocks((*place[1, -d], a1))
        a0, a1 = ways[0](a0), cross(a1, even) if d == -1 else ways[1](a1)
        if d != -1:
            d = -2 if d < 0 else 1
            (b0,), (b1,) = add_blocks((*place[0, d], b0)), add_blocks((*place[1, -d], b1))
            b0, b1 = ways[0](b0), ways[1](b1)
    sums = [near[place[s, 0][1]] for s in (0, 1)]
    theirs = swap((sums[1] + b1.astype(F32)).astype(BF16), "ylo").astype(F32)
    total = after(sums[0], query_grad) + a0.astype(F32) + a1.astype(F32) + b0.astype(F32) + theirs
    passage_grad = (total * slope(passage_act)).astype(BF16)
    return (query_grad, passage_grad)


def solution(mesh):
    split = Mesh(mesh.devices.reshape(2, 8, 2, 2, 4), ("ylo", "z", "core", "yhi", "x"))
    rows, columns = ("ylo", "z", "core"), ("yhi", "x")
    return jax.shard_map(
        shards,
        mesh=split,
        in_specs=(P(rows, columns), P(rows, columns), P(rows), P(rows)),
        out_specs=(P(rows, columns), P(rows, columns)),
        check_vma=False,
    )
```

```python
import functools
import math

import jax
import jax.numpy as jnp
from jax import lax
from jax.experimental import pallas as pl
from jax.experimental.pallas import tpu as pltpu
from jax.sharding import Mesh, PartitionSpec as P

VOCAB = 16384
REP = ("x", "yhi")
FACTOR = 8.0 / math.sqrt(VOCAB)
BF16, F32 = jnp.bfloat16, jnp.float32
ORDER = [4, 3, -3, 2, -2, 1, -1, 0]
KEYS = [(s, d) for d in ORDER for s in (0, 1)]
LATE = 4
VMEM = pl.BlockSpec(memory_space=pltpu.VMEM)
ANY = pl.BlockSpec(memory_space=pl.ANY)
PARAMS = pltpu.CompilerParams(vmem_limit_bytes=16 * 1024 * 1024)


def shape(dims, dtype):
    return jax.ShapeDtypeStruct(dims, dtype)


def saturate(act):
    wide = jnp.maximum(act.astype(F32), 0.0)
    small = wide - 0.5 * wide * wide
    return jnp.where(wide < 2.0**-8, small, jnp.log(1.0 + wide)).astype(BF16)


def slope(act):
    wide = act.astype(F32)
    return jnp.where(wide > 0.0, 1.0 / (1.0 + jnp.maximum(wide, 0.0)), 0.0)


def swap(value, axis):
    return lax.ppermute(value, axis, [(0, 1), (1, 0)])


def even(value):
    return lax.ppermute(value, "z", [(i, i ^ 1) for i in range(8)])


def odd(value):
    return lax.ppermute(value, "z", [(i, ((i - 1) ^ 1) + 1 & 7) for i in range(8)])


def cross(value, way):
    to = [i ^ 1 if way is even else ((i - 1) ^ 1) + 1 & 7 for i in range(8)]
    return lax.ppermute(value, ("ylo", "z"), [(y * 8 + i, (1 - y) * 8 + to[i]) for y in (0, 1) for i in range(8)])


def exchange(value):
    return lax.all_to_all(value, REP, split_axis=0, concat_axis=0)


def after(value, *others):
    return lax.optimization_barrier((value, *others))[0]


def early_kernel(mine_ref, other_ref, *refs):
    *blocks, part_ref, joined_ref = refs
    for i, block in enumerate(blocks):
        joined_ref[LATE * 32 + i * 32 : LATE * 32 + i * 32 + 32, :] = block[...]
    for i, ref in enumerate((mine_ref, other_ref)):
        for k in range(2):
            part_ref[i * 2 + k] = lax.dot_general(
                joined_ref[LATE * 32 :, :],
                ref[k * 256 : k * 256 + 256, :],
                (((1,), (1,)), ((), ())),
                preferred_element_type=F32,
            )


def score_kernel(mine_ref, other_ref, early_ref, _, *refs):
    *blocks, out_ref, joined_ref = refs
    for i, block in enumerate(blocks):
        joined_ref[i * 32 : i * 32 + 32, :] = block[...]
    for i, ref in enumerate((mine_ref, other_ref)):
        for k in range(2):
            early = early_ref[i * 2 + k]
            late = lax.dot_general(
                joined_ref[...],
                ref[k * 256 : k * 256 + 256, :],
                (((1,), (1,)), ((), ())),
                preferred_element_type=F32,
            )
            most = jnp.maximum(jnp.max(early, axis=0, keepdims=True), jnp.max(late, axis=0, keepdims=True))
            least = jnp.minimum(jnp.min(early, axis=0, keepdims=True), jnp.min(late, axis=0, keepdims=True))
            halves = jnp.round(most + least)
            centre = halves * 0.5
            reach = jnp.maximum(most - centre, centre - least)
            step = jnp.maximum(jnp.ceil(reach * (2.0**17 / 32767)), 1.0)
            scale = 2.0**17 / step
            row = lax.broadcasted_iota(jnp.int32, (16, 256), 0)
            extra = jnp.where(row == 0, halves, jnp.where(row == 1, step, 0.0))
            for n in range(2):
                columns = slice(n * 128, n * 128 + 128)
                at = i * 4 + k * 2 + n
                for start, part in ((0, late), (LATE * 32, early)):
                    code = jnp.round((part[:, columns] - centre[:, columns]) * scale[:, columns])
                    out_ref[at, start : start + part.shape[0], :] = code.astype(jnp.int32).astype(jnp.int16)
                out_ref[at, 512:, :] = extra[:, columns].astype(jnp.int32).astype(jnp.int16)


def partial_scores(mine, other, blocks):
    early, joined = pl.pallas_call(
        early_kernel,
        out_shape=(shape((4, 512 - LATE * 32, 256), F32), shape((512, 2048), BF16)),
        in_specs=[VMEM] * (18 - LATE),
        out_specs=(VMEM, VMEM),
        compiler_params=PARAMS,
    )(mine, other, *blocks[LATE:])
    return pl.pallas_call(
        score_kernel,
        out_shape=(shape((8, 528, 128), jnp.int16), shape((512, 2048), BF16)),
        grid=(1,),
        in_specs=[VMEM] * 3 + [ANY] + [VMEM] * LATE,
        out_specs=(VMEM, pl.BlockSpec((LATE * 32, 2048), lambda j: (0, 0))),
        input_output_aliases={3: 1},
        compiler_params=PARAMS,
    )(mine, other, early, joined, *blocks[:LATE])


def grad_kernel(pieces_ref, norm_ref, other_norm_ref, at_ref, other_at_ref, out_ref):
    core, y, z = lax.axis_index("core"), lax.axis_index("ylo"), lax.axis_index("z")
    rep = lax.axis_index("x") * 2 + lax.axis_index("yhi")
    norm = jnp.where(rep < 4, norm_ref[...], other_norm_ref[...])
    positive = jnp.where(rep < 4, at_ref[...], other_at_ref[...])
    turn = lax.broadcasted_iota(jnp.int32, (4, 128), 0) == lax.rem(rep, 4)
    norm = jnp.sum(jnp.where(turn, norm, 0.0), axis=0, keepdims=True)
    positive = jnp.sum(jnp.where(turn, positive, 0), axis=0, keepdims=True)
    scores = 0.0
    for k in range(8):
        extra = pieces_ref[k, 512:, :].astype(jnp.int32).astype(F32)
        code = pieces_ref[k, :512, :].astype(jnp.int32).astype(F32)
        scores = scores + (code * (extra[1:2] * 2.0**-17) + extra[0:1] * 0.5)
    place = lax.broadcasted_iota(jnp.int32, (512, 128), 0)
    turn = place >> 6
    ahead = jnp.where((turn & 1) == 0, 4 + (turn >> 1), (7 - turn) >> 1)
    ahead = jnp.where((z & 1) == 0, ahead, 8 - ahead)
    ident = ((y + (place >> 5)) & 1) * 512 + ((z + ahead) & 7) * 64 + core * 32 + (place & 31)
    onehot = (positive == ident).astype(F32)
    grad = (jnp.exp(scores * FACTOR - norm) - onehot) * (8.0 * FACTOR)
    grad = grad.astype(BF16)
    for k in range(8):
        out_ref[k] = grad


def score_grad(pieces, *rows):
    return pl.pallas_call(
        grad_kernel,
        out_shape=shape((8, 512, 128), BF16),
        in_specs=[VMEM] * 5,
        out_specs=VMEM,
        compiler_params=PARAMS,
    )(pieces, *rows)


def sum_kernel(at, sends, grad_ref, mine_ref, other_ref, *refs):
    out_ref, send_refs = refs[-1 - len(sends)], refs[len(refs) - len(sends) :]
    left = jnp.concatenate([grad_ref[k, at : at + 256, :] for k in range(8)], axis=1)
    for j in range(4):
        columns = slice(j * 512, j * 512 + 512)
        total = jnp.dot(left[:, :512], mine_ref[:, columns], preferred_element_type=F32)
        total += jnp.dot(left[:, 512:], other_ref[:, columns], preferred_element_type=F32)
        out_ref[:, :, columns] = total.reshape(8, 32, 512)
        for i, ref in zip(sends, send_refs):
            ref[:, columns] = total[i * 32 : i * 32 + 32].astype(BF16)


def passage_sums(grad, mine, other, at, sends):
    return pl.pallas_call(
        functools.partial(sum_kernel, at, sends),
        out_shape=(shape((8, 32, 2048), F32),) + (shape((32, 2048), BF16),) * len(sends),
        in_specs=[VMEM] * 3,
        out_specs=(VMEM,) * (1 + len(sends)),
        compiler_params=PARAMS,
    )(grad, mine, other)


def add_kernel(items, *refs):
    outs = refs[len(refs) - len(items) :]
    at = 0
    for (place, n), out in zip(items, outs):
        total = refs[at][place]
        for come in refs[at + 1 : at + 1 + n]:
            total = total + come[...].astype(F32)
        out[...] = total.astype(BF16)
        at += 1 + n


def add_blocks(*items):
    return pl.pallas_call(
        functools.partial(add_kernel, [(place, len(come)) for _, place, *come in items]),
        out_shape=(shape((32, 2048), BF16),) * len(items),
        in_specs=[VMEM] * sum(len(item) - 1 for item in items),
        out_specs=(VMEM,) * len(items),
        compiler_params=PARAMS,
    )(*[a for sums, _, *come in items for a in (sums, *come)])


def query_kernel(act_ref, own_grad_ref, other_grad_ref, own_ref, other_ref, out_ref, turned_ref):
    for i, g in enumerate((own_grad_ref, other_grad_ref)):
        for k in range(4):
            turned_ref[k * 128 : k * 128 + 128, i * 512 : i * 512 + 512] = g[k].T
    for j in range(4):
        columns = slice(j * 512, j * 512 + 512)
        total = jnp.dot(turned_ref[:, :512], own_ref[:, columns], preferred_element_type=F32)
        total += jnp.dot(turned_ref[:, 512:], other_ref[:, columns], preferred_element_type=F32)
        wide = act_ref[:, columns].astype(F32)
        below = 1.0 + jnp.maximum(wide, 0.0)
        guess = pl.reciprocal(below, approx=True)
        inverse = guess * (2.0 - below * guess)
        out_ref[:, columns] = jnp.where(wide > 0.0, total * inverse, 0.0).astype(BF16)


def query_grads(act, grad, other_grad, own, other):
    return pl.pallas_call(
        query_kernel,
        out_shape=shape((512, 2048), BF16),
        in_specs=[VMEM] * 5,
        out_specs=VMEM,
        scratch_shapes=[pltpu.VMEM((512, 1024), BF16)],
        compiler_params=PARAMS,
    )(act, grad[:4], other_grad, own, other)


def shards(query_act, passage_act, positive, normalizer):
    own = saturate(passage_act)
    blocks = {(0, 0): own, (1, 0): swap(own, "ylo")}
    for d in range(1, 4):
        for s in (0, 1):
            blocks[s, d], blocks[s, -d] = even(blocks[s, 1 - d]), odd(blocks[s, d - 1])
    blocks[0, 4], blocks[1, 4] = even(blocks[0, -3]), odd(blocks[1, 3])

    mine = saturate(query_act)
    other = swap(mine, "core")
    norm, other_norm = normalizer.reshape(4, 128), swap(normalizer, "core").reshape(4, 128)
    at, other_at = positive.reshape(4, 128), swap(positive, "core").reshape(4, 128)
    blocks[0, 4], norm, other_norm, at, other_at = lax.optimization_barrier(
        (blocks[0, 4], norm, other_norm, at, other_at)
    )

    part, joined = partial_scores(mine, other, [blocks[k] for k in KEYS])
    grad = exchange(score_grad(exchange(part), norm, other_norm, at, other_at))

    joined = after(joined, grad)
    query_grad = query_grads(query_act, grad, swap(grad[4:], "core"), joined, swap(joined, "core"))

    far, a0, a1, b0, b1 = passage_sums(grad, mine, other, 0, [1, 0, 3, 4])
    (near,) = passage_sums(grad, mine, other, 256, [])
    place = {k: (far, i) if i < 8 else (near, i - 8) for i, k in enumerate(KEYS)}
    a0, a1, b0, b1 = even(a0), odd(a1), even(b0), odd(b1)
    for d in (-3, 2, -1):
        ways = (odd, even) if d < 0 else (even, odd)
        (a0,), (a1,) = add_blocks((*place[1, d], a0)), add_blocks((*place[0, -d], a1))
        a0, a1 = cross(a0, odd) if d == -1 else ways[0](a0), ways[1](a1)
        if d != -1:
            d = -2 if d < 0 else 1
            (b0,), (b1,) = add_blocks((*place[1, d], b0)), add_blocks((*place[0, -d], b1))
            b0, b1 = ways[0](b0), ways[1](b1)
    sums = [near[place[s, 0][1]] for s in (0, 1)]
    theirs = swap((sums[1] + b0.astype(F32)).astype(BF16), "ylo").astype(F32)
    total = after(sums[0], query_grad) + a0.astype(F32) + a1.astype(F32) + b1.astype(F32) + theirs
    passage_grad = (total * slope(passage_act)).astype(BF16)
    return (query_grad, passage_grad)


def solution(mesh):
    split = Mesh(mesh.devices.reshape(2, 8, 2, 2, 4), ("ylo", "z", "core", "yhi", "x"))
    rows, columns = ("ylo", "z", "core"), ("yhi", "x")
    return jax.shard_map(
        shards,
        mesh=split,
        in_specs=(P(rows, columns), P(rows, columns), P(rows), P(rows)),
        out_specs=(P(rows, columns), P(rows, columns)),
        check_vma=False,
    )
```

```python
import functools
import math

import jax
import jax.numpy as jnp
from jax import lax
from jax.experimental import pallas as pl
from jax.experimental.pallas import tpu as pltpu
from jax.sharding import Mesh, PartitionSpec as P

VOCAB = 16384
REP = ("x", "yhi")
FACTOR = 8.0 / math.sqrt(VOCAB)
BF16, F32 = jnp.bfloat16, jnp.float32
ORDER = [4, 3, -3, 2, -2, 1, -1, 0]
KEYS = [(s, d) for d in ORDER for s in (0, 1)]
LATE = 3
VMEM = pl.BlockSpec(memory_space=pltpu.VMEM)
ANY = pl.BlockSpec(memory_space=pl.ANY)
PARAMS = pltpu.CompilerParams(vmem_limit_bytes=16 * 1024 * 1024)


def shape(dims, dtype):
    return jax.ShapeDtypeStruct(dims, dtype)


def saturate(act):
    wide = jnp.maximum(act.astype(F32), 0.0)
    small = wide - 0.5 * wide * wide
    return jnp.where(wide < 2.0**-8, small, jnp.log(1.0 + wide)).astype(BF16)


def slope(act):
    wide = act.astype(F32)
    return jnp.where(wide > 0.0, 1.0 / (1.0 + jnp.maximum(wide, 0.0)), 0.0)


def swap(value, axis):
    return lax.ppermute(value, axis, [(0, 1), (1, 0)])


def even(value):
    return lax.ppermute(value, "z", [(i, i ^ 1) for i in range(8)])


def odd(value):
    return lax.ppermute(value, "z", [(i, ((i - 1) ^ 1) + 1 & 7) for i in range(8)])


def cross(value, way):
    to = [i ^ 1 if way is even else ((i - 1) ^ 1) + 1 & 7 for i in range(8)]
    return lax.ppermute(value, ("ylo", "z"), [(y * 8 + i, (1 - y) * 8 + to[i]) for y in (0, 1) for i in range(8)])


def exchange(value):
    return lax.all_to_all(value, REP, split_axis=0, concat_axis=0)


def after(value, *others):
    return lax.optimization_barrier((value, *others))[0]


def early_kernel(mine_ref, other_ref, *refs):
    *blocks, part_ref, joined_ref = refs
    for i, block in enumerate(blocks):
        joined_ref[LATE * 32 + i * 32 : LATE * 32 + i * 32 + 32, :] = block[...]
    for i, ref in enumerate((mine_ref, other_ref)):
        for k in range(2):
            part_ref[i * 2 + k] = lax.dot_general(
                joined_ref[LATE * 32 :, :],
                ref[k * 256 : k * 256 + 256, :],
                (((1,), (1,)), ((), ())),
                preferred_element_type=F32,
            )


def score_kernel(mine_ref, other_ref, early_ref, _, *refs):
    *blocks, out_ref, joined_ref = refs
    for i, block in enumerate(blocks):
        joined_ref[i * 32 : i * 32 + 32, :] = block[...]
    for i, ref in enumerate((mine_ref, other_ref)):
        for k in range(2):
            early = early_ref[i * 2 + k]
            late = lax.dot_general(
                joined_ref[...],
                ref[k * 256 : k * 256 + 256, :],
                (((1,), (1,)), ((), ())),
                preferred_element_type=F32,
            )
            most = jnp.maximum(jnp.max(early, axis=0, keepdims=True), jnp.max(late, axis=0, keepdims=True))
            least = jnp.minimum(jnp.min(early, axis=0, keepdims=True), jnp.min(late, axis=0, keepdims=True))
            halves = jnp.round(most + least)
            centre = halves * 0.5
            reach = jnp.maximum(most - centre, centre - least)
            step = jnp.maximum(jnp.ceil(reach * (2.0**17 / 32767)), 1.0)
            scale = 2.0**17 / step
            row = lax.broadcasted_iota(jnp.int32, (16, 256), 0)
            extra = jnp.where(row == 0, halves, jnp.where(row == 1, step, 0.0))
            for n in range(2):
                columns = slice(n * 128, n * 128 + 128)
                at = i * 4 + k * 2 + n
                for start, part in ((0, late), (LATE * 32, early)):
                    code = jnp.round((part[:, columns] - centre[:, columns]) * scale[:, columns])
                    out_ref[at, start : start + part.shape[0], :] = code.astype(jnp.int32).astype(jnp.int16)
                out_ref[at, 512:, :] = extra[:, columns].astype(jnp.int32).astype(jnp.int16)


def partial_scores(mine, other, blocks):
    early, joined = pl.pallas_call(
        early_kernel,
        out_shape=(shape((4, 512 - LATE * 32, 256), F32), shape((512, 2048), BF16)),
        in_specs=[VMEM] * (18 - LATE),
        out_specs=(VMEM, VMEM),
        compiler_params=PARAMS,
    )(mine, other, *blocks[LATE:])
    return pl.pallas_call(
        score_kernel,
        out_shape=(shape((8, 528, 128), jnp.int16), shape((512, 2048), BF16)),
        grid=(1,),
        in_specs=[VMEM] * 3 + [ANY] + [VMEM] * LATE,
        out_specs=(VMEM, pl.BlockSpec((LATE * 32, 2048), lambda j: (0, 0))),
        input_output_aliases={3: 1},
        compiler_params=PARAMS,
    )(mine, other, early, joined, *blocks[:LATE])


def grad_kernel(pieces_ref, norm_ref, other_norm_ref, at_ref, other_at_ref, out_ref):
    core, y, z = lax.axis_index("core"), lax.axis_index("ylo"), lax.axis_index("z")
    rep = lax.axis_index("x") * 2 + lax.axis_index("yhi")
    norm = jnp.where(rep < 4, norm_ref[...], other_norm_ref[...])
    positive = jnp.where(rep < 4, at_ref[...], other_at_ref[...])
    turn = lax.broadcasted_iota(jnp.int32, (4, 128), 0) == lax.rem(rep, 4)
    norm = jnp.sum(jnp.where(turn, norm, 0.0), axis=0, keepdims=True)
    positive = jnp.sum(jnp.where(turn, positive, 0), axis=0, keepdims=True)
    scores = 0.0
    for k in range(8):
        extra = pieces_ref[k, 512:, :].astype(jnp.int32).astype(F32)
        code = pieces_ref[k, :512, :].astype(jnp.int32).astype(F32)
        scores = scores + (code * (extra[1:2] * 2.0**-17) + extra[0:1] * 0.5)
    place = lax.broadcasted_iota(jnp.int32, (512, 128), 0)
    turn = place >> 6
    ahead = jnp.where((turn & 1) == 0, 4 + (turn >> 1), (7 - turn) >> 1)
    ahead = jnp.where((z & 1) == 0, ahead, 8 - ahead)
    ident = ((y + (place >> 5)) & 1) * 512 + ((z + ahead) & 7) * 64 + core * 32 + (place & 31)
    onehot = (positive == ident).astype(F32)
    grad = (jnp.exp(scores * FACTOR - norm) - onehot) * (8.0 * FACTOR)
    grad = grad.astype(BF16)
    for k in range(8):
        out_ref[k] = grad


def score_grad(pieces, *rows):
    return pl.pallas_call(
        grad_kernel,
        out_shape=shape((8, 512, 128), BF16),
        in_specs=[VMEM] * 5,
        out_specs=VMEM,
        compiler_params=PARAMS,
    )(pieces, *rows)


def sum_kernel(at, sends, grad_ref, mine_ref, other_ref, *refs):
    out_ref, send_refs = refs[-1 - len(sends)], refs[len(refs) - len(sends) :]
    left = jnp.concatenate([grad_ref[k, at : at + 256, :] for k in range(8)], axis=1)
    for j in range(4):
        columns = slice(j * 512, j * 512 + 512)
        total = jnp.dot(left[:, :512], mine_ref[:, columns], preferred_element_type=F32)
        total += jnp.dot(left[:, 512:], other_ref[:, columns], preferred_element_type=F32)
        out_ref[:, :, columns] = total.reshape(8, 32, 512)
        for i, ref in zip(sends, send_refs):
            ref[:, columns] = total[i * 32 : i * 32 + 32].astype(BF16)


def passage_sums(grad, mine, other, at, sends):
    return pl.pallas_call(
        functools.partial(sum_kernel, at, sends),
        out_shape=(shape((8, 32, 2048), F32),) + (shape((32, 2048), BF16),) * len(sends),
        in_specs=[VMEM] * 3,
        out_specs=(VMEM,) * (1 + len(sends)),
        compiler_params=PARAMS,
    )(grad, mine, other)


def add_kernel(items, *refs):
    outs = refs[len(refs) - len(items) :]
    at = 0
    for (place, n), out in zip(items, outs):
        total = refs[at][place]
        for come in refs[at + 1 : at + 1 + n]:
            total = total + come[...].astype(F32)
        out[...] = total.astype(BF16)
        at += 1 + n


def add_blocks(*items):
    return pl.pallas_call(
        functools.partial(add_kernel, [(place, len(come)) for _, place, *come in items]),
        out_shape=(shape((32, 2048), BF16),) * len(items),
        in_specs=[VMEM] * sum(len(item) - 1 for item in items),
        out_specs=(VMEM,) * len(items),
        compiler_params=PARAMS,
    )(*[a for sums, _, *come in items for a in (sums, *come)])


def query_kernel(act_ref, own_grad_ref, other_grad_ref, own_ref, other_ref, out_ref, turned_ref, held_ref, sems):
    copies = []
    for i, g in enumerate((own_grad_ref, other_grad_ref)):
        for k in range(4):
            turned_ref[k * 128 : k * 128 + 128, i * 512 : i * 512 + 512] = g[k].T
    for j in range(4):
        columns = slice(j * 512, j * 512 + 512)
        total = jnp.dot(turned_ref[:, :512], own_ref[:, columns], preferred_element_type=F32)
        total += jnp.dot(turned_ref[:, 512:], other_ref[:, columns], preferred_element_type=F32)
        wide = act_ref[:, columns].astype(F32)
        below = 1.0 + jnp.maximum(wide, 0.0)
        guess = pl.reciprocal(below, approx=True)
        inverse = guess * (2.0 - below * guess)
        held_ref[:, columns] = jnp.where(wide > 0.0, total * inverse, 0.0).astype(BF16)
        copies.append(pltpu.make_async_copy(held_ref.at[:, columns], out_ref.at[:, columns], sems.at[j]))
        copies[-1].start()
    for copy in copies:
        copy.wait()


def query_grads(act, grad, other_grad, own, other):
    return pl.pallas_call(
        query_kernel,
        out_shape=shape((512, 2048), BF16),
        in_specs=[VMEM] * 5,
        out_specs=ANY,
        scratch_shapes=[
            pltpu.VMEM((512, 1024), BF16),
            pltpu.VMEM((512, 2048), BF16),
            pltpu.SemaphoreType.DMA((4,)),
        ],
        compiler_params=PARAMS,
    )(act, grad[:4], other_grad, own, other)


def shards(query_act, passage_act, positive, normalizer):
    own = saturate(passage_act)
    blocks = {(0, 0): own, (1, 0): swap(own, "ylo")}
    for d in range(1, 4):
        for s in (0, 1):
            blocks[s, d], blocks[s, -d] = even(blocks[s, 1 - d]), odd(blocks[s, d - 1])
    blocks[0, 4], blocks[1, 4] = even(blocks[0, -3]), odd(blocks[1, 3])

    mine = saturate(query_act)
    other = swap(mine, "core")
    norm, other_norm = normalizer.reshape(4, 128), swap(normalizer, "core").reshape(4, 128)
    at, other_at = positive.reshape(4, 128), swap(positive, "core").reshape(4, 128)
    blocks[0, 4], norm, other_norm, at, other_at = lax.optimization_barrier(
        (blocks[0, 4], norm, other_norm, at, other_at)
    )

    part, joined = partial_scores(mine, other, [blocks[k] for k in KEYS])
    grad = exchange(score_grad(exchange(part), norm, other_norm, at, other_at))

    joined = after(joined, grad)
    query_grad = query_grads(query_act, grad, swap(grad[4:], "core"), joined, swap(joined, "core"))

    far, a0, a1, b0, b1 = passage_sums(grad, mine, other, 0, [1, 0, 3, 4])
    (near,) = passage_sums(grad, mine, other, 256, [])
    place = {k: (far, i) if i < 8 else (near, i - 8) for i, k in enumerate(KEYS)}
    a0, a1, b0, b1 = even(a0), odd(a1), even(b0), odd(b1)
    for d in (-3, 2, -1):
        ways = (odd, even) if d < 0 else (even, odd)
        (a1,), (a0,) = add_blocks((*place[0, -d], a1)), add_blocks((*place[1, d], a0))
        a1, a0 = ways[1](a1), cross(a0, odd) if d == -1 else ways[0](a0)
        if d != -1:
            d = -2 if d < 0 else 1
            (b0,), (b1,) = add_blocks((*place[1, d], b0)), add_blocks((*place[0, -d], b1))
            b0, b1 = ways[0](b0), ways[1](b1)
    sums = [near[place[s, 0][1]] for s in (0, 1)]
    theirs = swap((sums[1] + b0.astype(F32)).astype(BF16), "ylo").astype(F32)
    total = after(sums[0], query_grad) + a0.astype(F32) + a1.astype(F32) + b1.astype(F32) + theirs
    passage_grad = (total * slope(passage_act)).astype(BF16)
    return (query_grad, passage_grad)


def solution(mesh):
    split = Mesh(mesh.devices.reshape(2, 8, 2, 2, 4), ("ylo", "z", "core", "yhi", "x"))
    rows, columns = ("ylo", "z", "core"), ("yhi", "x")
    return jax.shard_map(
        shards,
        mesh=split,
        in_specs=(P(rows, columns), P(rows, columns), P(rows), P(rows)),
        out_specs=(P(rows, columns), P(rows, columns)),
        check_vma=False,
    )
```
